512 devices in a mesh: mode: 32 (over y, x, core), space: 16 (over z).
Axes of the slice: x: 4, y: 4, z: 16, core: 2. Of those that a mesh axis runs over, the one named last changes fastest.
Arguments:
- mode_field: bfloat16 [288, 128, 8, 128], P('mode', 'space'), may hold values from -6 to 6
- kl_coeff: float32 [11, 128, 8, 128], P(None, 'space'), may hold values from -4 to 4
- mode_slot: int32 [286], replicated, may hold values from 0 to 287, as said below
- trip_kl: int32 [1606], replicated, may hold values from 0 to 10, as said below
- trip_in: int32 [1606], replicated, may hold values from 0 to 285
- trip_out: int32 [1606], replicated, may hold values from 0 to 285, as said below
- trip_weight: bfloat16 [1606], replicated, may hold values from 1 to 2
Outputs:
- response: float32 [288, 128, 8, 128], P('mode', 'space')
The draws below stay inside these ranges and needn't reach their ends.
Inputs may be any that keep to these rules, and one draw needn't show every extreme that they name: `mode_slot`: the 286 modes sit in distinct slots. `trip_kl`: each entry names a distinct triple of expansion term, input mode and output mode. `trip_out`: every mode is the output mode of some entry.
All inputs are finite; a program needn't handle non-finite values.
Results may differ from the reference program's by a relative error of at most 0.0003.
Values may be sent and summed in bfloat16 or wider, within the bound.
A program may use at most 64 MiB of HBM per device.

```python
import math
import jax
import jax.numpy as jnp
import numpy as np
from jax import lax

KL = 11
MODES = 286
NTRIP = 1606
NX = 128
NY = 8
SLOTS_ALL = 288
NZ = 128


def multi_indices(dim_count, degree):
    if dim_count == 0:
        return [()]
    result = []
    for leading in range(degree + 1):
        for remainder in multi_indices(dim_count - 1, degree - leading):
            result.append((leading,) + remainder)
    return result


def chaos_triples(dim_count, degree):
    basis = multi_indices(dim_count, degree)
    position = {alpha: number for number, alpha in enumerate(basis)}
    kl_list = []
    in_list = []
    out_list = []
    weight_list = []
    for alpha in basis:
        kl_list.append(0)
        in_list.append(position[alpha])
        out_list.append(position[alpha])
        weight_list.append(1.0)
    for alpha in basis:
        if sum(alpha) < degree:
            for axis_number in range(dim_count):
                raised = tuple((alpha[slot_dim] + (1 if slot_dim == axis_number else 0) for slot_dim in range(dim_count)))
                factor = math.sqrt(alpha[axis_number] + 1.0)
                kl_list.append(axis_number + 1)
                in_list.append(position[alpha])
                out_list.append(position[raised])
                weight_list.append(factor)
                kl_list.append(axis_number + 1)
                in_list.append(position[raised])
                out_list.append(position[alpha])
                weight_list.append(factor)
    return (np.array(kl_list, np.int32), np.array(in_list, np.int32), np.array(out_list, np.int32), np.array(weight_list, np.float32))


def triple_draw(key):
    kl_ids, in_ids, out_ids, factors = chaos_triples(KL - 1, 3)
    relabel = jax.random.permutation(jax.random.fold_in(key, 101), MODES).astype(jnp.int32)
    order = jax.random.permutation(jax.random.fold_in(key, 102), NTRIP)
    kl_part = jnp.asarray(kl_ids)[order]
    in_part = relabel[jnp.asarray(in_ids)][order]
    out_part = relabel[jnp.asarray(out_ids)][order]
    weight_part = jnp.asarray(factors, jnp.float32)[order]
    return (kl_part, in_part, out_part, weight_part)


def draw_trip_kl(key, part):
    return triple_draw(key)[0]


def draw_trip_in(key, part):
    return triple_draw(key)[1]


def draw_trip_out(key, part):
    return triple_draw(key)[2]


def draw_trip_weight(key, part):
    return triple_draw(key)[3].astype(jnp.bfloat16)


def draw_mode_slot(key, part):
    key = jax.random.fold_in(key, 3)
    first_key, second_key = jax.random.split(key)
    spare_slots = 1 + jax.random.permutation(first_key, SLOTS_ALL - 2)[:SLOTS_ALL - MODES]
    empty_flags = jnp.zeros((SLOTS_ALL,), jnp.int32).at[spare_slots].set(1)
    sort_keys = empty_flags * SLOTS_ALL + jnp.arange(SLOTS_ALL, dtype=jnp.int32)
    used_slots = jnp.argsort(sort_keys, stable=True)[:MODES].astype(jnp.int32)
    return jax.random.permutation(second_key, used_slots)


def draw_kl_coeff(key, part):
    key = jax.random.fold_in(key, 7)
    mean_key, term_key = jax.random.split(key)
    term_shape = (KL - 1, NZ, NY, NX)
    mean_field = jnp.exp(jax.random.uniform(mean_key, (1, NZ, NY, NX), jnp.float32, -0.7, 0.7))
    rough_part = jnp.clip(jax.random.normal(term_key, term_shape, jnp.float32), -3.0, 3.0)
    decay_scale = 0.6 * 0.85 ** jnp.arange(KL - 1, dtype=jnp.float32)
    return jnp.concatenate([mean_field, mean_field * decay_scale[:, None, None, None] * rough_part], axis=0)


def steps_of(rng, shape, cuts, least, high):
    gain = 1.0
    for dim, shards_of in cuts:
        steps = jax.random.uniform(jax.random.fold_in(jax.random.fold_in(rng, 6), dim), (shards_of,), jnp.float32, least / len(cuts), high / len(cuts))
        gain = gain * jnp.repeat(jnp.exp(steps), shape[dim] // shards_of).reshape((-1,) + (1,) * (len(shape) - 1 - dim))
    return gain


def noise(rng, dims, deviation, most, cuts=(), kind=jnp.bfloat16):
    values = deviation * jax.random.normal(rng, dims, jnp.float32)
    if cuts:
        values = values * steps_of(rng, dims, cuts, -0.22, 0.18)
    return jnp.clip(values, -most, most).astype(kind)


def setup_inputs(seed: int = 0) -> dict:
    seeds = jax.random.split(jax.random.key(seed), 8)
    return {
        "mode_field": noise(seeds[0], (SLOTS_ALL, NZ, NY, NX), 1.0, 6.0, ((0, 32), (1, 16))),
        "kl_coeff": draw_kl_coeff(jax.random.fold_in(seeds[7], 71), 0),
        "mode_slot": draw_mode_slot(jax.random.fold_in(seeds[7], 71), 0),
        "trip_kl": draw_trip_kl(jax.random.fold_in(seeds[7], 71), 0),
        "trip_in": draw_trip_in(jax.random.fold_in(seeds[7], 71), 0),
        "trip_out": draw_trip_out(jax.random.fold_in(seeds[7], 71), 0),
        "trip_weight": draw_trip_weight(jax.random.fold_in(seeds[7], 71), 0),
    }


neighbour_steps = ((1, 0, 0), (-1, 0, 0), (0, 1, 0), (0, -1, 0), (0, 0, 1), (0, 0, -1))


def shifted(values, step_z, step_y, step_x):
    plane_count = values.shape[-3]
    row_count = values.shape[-2]
    col_count = values.shape[-1]
    return values[..., 1 + step_z:plane_count - 1 + step_z, 1 + step_y:row_count - 1 + step_y, 1 + step_x:col_count - 1 + step_x]


def diffusion(values, coeffs):
    centre_value = shifted(values, 0, 0, 0)
    centre_coeff = shifted(coeffs, 0, 0, 0)
    running = jnp.zeros(centre_value.shape, jnp.float32)
    for step_z, step_y, step_x in neighbour_steps:
        face_value = 0.5 * (centre_coeff + shifted(coeffs, step_z, step_y, step_x))
        running = running + face_value * (centre_value - shifted(values, step_z, step_y, step_x))
    return running


def reference(mode_field, kl_coeff, mode_slot, trip_kl, trip_in, trip_out, trip_weight):
    coeff_pad = jnp.pad(kl_coeff, ((0, 0), (1, 1), (1, 1), (1, 1)))
    slot_in = mode_slot[trip_in].astype(jnp.int32)
    slot_out = mode_slot[trip_out].astype(jnp.int32)
    term_ids = trip_kl.astype(jnp.int32)
    weights = trip_weight.astype(jnp.float32)

    def add_one(trip_index, running):
        source = lax.dynamic_index_in_dim(mode_field, slot_in[trip_index], 0, keepdims=False).astype(jnp.float32)
        coeffs = lax.dynamic_index_in_dim(coeff_pad, term_ids[trip_index], 0, keepdims=False)
        applied = diffusion(jnp.pad(source, 1), coeffs)
        target = slot_out[trip_index]
        current = lax.dynamic_index_in_dim(running, target, 0, keepdims=True)
        return lax.dynamic_update_index_in_dim(running, current + weights[trip_index] * applied[None], target, 0)

    start_total = jnp.zeros(mode_field.shape, jnp.float32)
    return lax.fori_loop(0, NTRIP, add_one, start_total)
```

```python
import jax
import jax.numpy as jnp
from jax import lax
from jax.experimental import pallas as pl
from jax.experimental.pallas import tpu as pltpu
from jax.sharding import PartitionSpec as P

MESH = pl.DeviceIdType.MESH
F32 = jnp.float32
BF16 = jnp.bfloat16
NT = (((1,), (1,)), ((), ()))

SIDE = 4
CHIPS = 16
DEVICES = 32
OWN = 9
TERMS = 11
TRIPS = 1606
TRIPS_PAD = 1664
MODES = 286
ROWS = 144
KPAD = 384
MSG = 48
ANS = 40


def iota(shape, dim):
    return lax.broadcasted_iota(jnp.int32, shape, dim)


def lane_of(value):
    return iota(value.shape, value.ndim - 1)


def split(value, parts):
    out = []
    for _ in range(parts):
        piece = value.astype(BF16)
        out.append(piece)
        value = value - piece.astype(F32)
    return out


def yz_sum(value):
    lane = lane_of(value)
    y = lane % 8
    z = (lane // 8) % 8
    total = jnp.where(y > 0, pltpu.roll(value, 1, 1), 0.0)
    total = total + jnp.where(y < 7, pltpu.roll(value, 127, 1), 0.0)
    total = total + jnp.where(z > 0, pltpu.roll(value, 8, 1), 0.0)
    return total + jnp.where(z < 7, pltpu.roll(value, 120, 1), 0.0)


def x_sum(tiles, j):
    lane = lane_of(tiles(0))
    left = tiles(j - 1) if j > 0 else jnp.where(lane >= 64, pltpu.roll(tiles(3), 64, 1), 0.0)
    right = tiles(j + 1) if j < 3 else jnp.where(lane < 64, pltpu.roll(tiles(0), 64, 1), 0.0)
    return left + right


def column_select(rows, chip, half, j):
    target = 8 * chip + j + 4 * half
    target = jnp.where(j == 4, jnp.where(half == 0, 8 * chip - 1, 8 * chip + 8), target)
    target = jnp.where(j > 4, -1, target)
    return jnp.where(iota((rows, 128), 1) == target, 1.0, 0.0).astype(BF16)


def edge_gather():
    row = iota((512, 128), 0)
    out = iota((512, 128), 1)
    j, half, z, y = row // 128, (row // 64) % 2, (row // 8) % 8, row % 8
    place = (j + 4 * half) * 8 + y
    hit = ((z == 0) & (out == place)) | ((z == 7) & (out == 64 + place))
    return jnp.where(hit, 1.0, 0.0).astype(BF16)


def edge_spread():
    out = iota((128, 512), 1)
    row = iota((128, 512), 0)
    j, half, z, y = out // 128, (out // 64) % 2, (out // 8) % 8, out % 8
    place = (j + 4 * half) * 8 + y
    hit = ((z == 7) & (row == place)) | ((z == 0) & (row == 64 + place))
    return jnp.where(hit, 1.0, 0.0).astype(BF16)


def kernel(
    v_ref, k_ref, slot_ref, kl_ref, in_ref, out_ref, w_ref, o_ref,
    pack, msg, got, ninth, vf, vb, svb, onehot, cc, wbuf, ubuf, hbuf,
    kt, ka, eok, kzi, hxc, hzc, eo, ezi, ra, bb, ex, ez, ans, ret, turn, places, trip, table,
    send1, recv1, sendk, recvk, sendz, recvz, send2, recv2,
):
    me = lax.axis_index("mode")
    zi = lax.axis_index("space")
    nz = lax.axis_size("space")
    chip, core = me // 2, me % 2
    ypos, xpos = chip // SIDE, chip % SIDE

    offsets = [
        (ky, kx, kc) for ky in range(SIDE) for kx in range(SIDE) for kc in range(2) if (ky, kx, kc) != (0, 0, 0)
    ]
    offsets.sort(key=lambda o: -(min(o[0], SIDE - o[0]) + min(o[1], SIDE - o[1])))

    def chip_at(ky, kx):
        return lax.rem(ypos + ky, SIDE) * SIDE + lax.rem(xpos + kx, SIDE)

    up, down = lax.rem(zi + 1, nz), lax.rem(zi + nz - 1, nz)

    barrier = pltpu.get_barrier_semaphore()
    for ky, kx, kc in offsets:
        pl.semaphore_signal(
            barrier, inc=1, device_id=(chip_at(ky, kx) * 2 + lax.rem(core + kc, 2), zi), device_id_type=MESH
        )
    for other in (up, down):
        pl.semaphore_signal(barrier, inc=1, device_id=(me, other), device_id_type=MESH)

    row = iota((256, 128), 0)
    select = column_select(256, (row % 128) // 8, row // 128, row % 8)
    low = iota((128, 128), 1) < 64
    for m in range(OWN):
        field = v_ref[m].astype(F32).reshape(64, 128)
        field = jnp.concatenate([field, field], axis=0).astype(BF16)
        turned = lax.dot_general(select, field, NT, preferred_element_type=F32)
        turned = jnp.where(low, turned[:128], turned[128:])
        for c in range(CHIPS):
            if m < 8:
                pack[pl.ds(c * 64 + m, 8, stride=8), :] = turned[c * 8 : c * 8 + 8]
            else:
                pack[pl.ds(c * 64 + 40, 8), :] = turned[c * 8 : c * 8 + 8]
    for c in range(CHIPS):
        msg[c] = pack[pl.ds(c * 64, MSG), :].astype(BF16)
    got[pl.ds(me, 1)] = msg[pl.ds(chip, 1)]

    pl.semaphore_wait(barrier, len(offsets) + 2)
    for ky, kx, kc in offsets:
        target = chip_at(ky, kx)
        pltpu.make_async_remote_copy(
            src_ref=msg.at[target], dst_ref=got.at[me], send_sem=send1, recv_sem=recv1,
            device_id=(target * 2 + lax.rem(core + kc, 2), zi), device_id_type=MESH,
        ).start()

    gather_edge = edge_gather()
    spread_edge = edge_spread()
    kt[...] = jnp.zeros_like(kt)
    row16 = iota((16, 128), 0)
    select_k = column_select(16, chip, row16 // 8, row16 % 8)
    for i in range(TERMS):
        block = k_ref[i].reshape(64, 128)
        block = jnp.concatenate([block, block], axis=0)
        turned = jnp.zeros((16, 128), F32)
        for piece in reversed(split(block, 3)):
            turned = turned + lax.dot_general(select_k, piece, NT, preferred_element_type=F32)
        kt[pl.ds(i, 8, stride=16), :] = jnp.where(low[:8], turned[:8], turned[8:])

    def k_tile(j):
        return kt[j * 16 : j * 16 + 16, :]

    whole = jnp.concatenate([k_tile(j) for j in range(4)], axis=1)
    edge = jnp.zeros((16, 128), F32)
    for piece in reversed(split(whole, 3)):
        edge = edge + jnp.dot(piece, gather_edge, preferred_element_type=F32)
    eok[...] = edge
    k_copies = []
    for n, other in enumerate((down, up)):
        copy = pltpu.make_async_remote_copy(
            src_ref=eok, dst_ref=kzi.at[n], send_sem=sendk.at[n], recv_sem=recvk.at[n],
            device_id=(me, other), device_id_type=MESH,
        )
        copy.start()
        k_copies.append(copy)

    trip[...] = jnp.full(trip.shape, -1, jnp.int32)
    trip[0:1, 0:TRIPS] = in_ref[...]
    trip[1:2, 0:TRIPS] = out_ref[...]
    trip[2:3, 0:TRIPS] = kl_ref[...]
    table[...] = jnp.zeros(table.shape, F32)
    table[0:1, 0:TRIPS] = w_ref[...].astype(F32)
    slots = jnp.broadcast_to(slot_ref[...], (16, MODES))
    dev = lax.shift_right_logical(slots * 57, 9)
    kind = slots - dev * OWN
    column = jnp.where(kind < 8, dev * 8 + kind, 256 + dev)
    place = jnp.where(kind < 8, (dev // 2) * 8 + kind, 128 + dev // 2)
    place = jnp.where(dev % 2 == core, place, 240)
    row16m = iota((16, MODES), 0)
    number = jnp.where(row16m < 2, column, place)
    digits = jnp.where(row16m % 2 == 0, lax.shift_right_logical(number, 4), number & 15)
    digits = jnp.where(row16m < 4, digits, 0).astype(F32)
    places[...] = jnp.zeros((16, KPAD), F32)
    places[:, 0:MODES] = digits
    digits = places[...].astype(BF16)
    mode_row = iota((KPAD, TRIPS_PAD), 0)
    hit_in = jnp.where(mode_row == trip[0:1, :], 1.0, 0.0).astype(BF16)
    look_in = jnp.dot(digits, hit_in, preferred_element_type=F32)
    hit_out = jnp.where(mode_row == trip[1:2, :], 1.0, 0.0).astype(BF16)
    look_out = jnp.dot(digits, hit_out, preferred_element_type=F32)
    column_t = (look_in[0:1] * 16.0 + look_in[1:2]).astype(jnp.int32)
    place_t = (look_out[2:3] * 16.0 + look_out[3:4]).astype(jnp.int32)
    key_t = jnp.where(place_t < ROWS, trip[2:3, :] * ROWS + place_t, -1)
    trip[3:4, :] = key_t
    by_column = jnp.where(mode_row == column_t, 1.0, 0.0).astype(BF16)

    @pl.loop(0, TERMS)
    def _(i):
        rows = iota((ROWS, TRIPS_PAD), 0) + i * ROWS
        part = jnp.where(rows == trip[3:4, :], table[0:1, :], 0.0).astype(BF16)
        onehot[pl.ds(pl.multiple_of(i * ROWS, 16), ROWS), :] = part

    coupling = lax.dot_general(onehot[...], by_column, NT, preferred_element_type=F32).astype(BF16)
    cc[:, 0:KPAD] = coupling
    cc[:, KPAD:] = coupling

    for copy in k_copies:
        copy.wait()
    lane16 = iota((16, 128), 1)
    inside_up = jnp.where(zi < nz - 1, 1.0, 0.0)
    inside_down = jnp.where(zi > 0, 1.0, 0.0)
    k_beyond = jnp.where(lane16 < 64, kzi[0] * inside_up, kzi[1] * inside_down)
    hzc[...] = pltpu.roll(edge, 64, 1) + k_beyond
    hxc[...] = jnp.where(lane16 < 64, k_tile(0), k_tile(3)) + k_tile(4)
    spread = jnp.zeros((16, 512), F32)
    for piece in reversed(split(k_beyond, 3)):
        spread = spread + jnp.dot(piece, spread_edge, preferred_element_type=F32)
    for j in range(4):
        total = 6.0 * k_tile(j) + x_sum(k_tile, j) + yz_sum(k_tile(j)) + spread[:, j * 128 : j * 128 + 128]
        if j == 0:
            total = total + jnp.where(lane16 < 64, k_tile(4), 0.0)
        if j == 3:
            total = total + jnp.where(lane16 >= 64, k_tile(4), 0.0)
        ka[j] = total

    vb[288:KPAD, :] = jnp.zeros((KPAD - 288, 768), BF16)
    svb[288:KPAD, :] = jnp.zeros((KPAD - 288, 512), BF16)
    svb[KPAD + 288 :, :] = jnp.zeros((KPAD - 288, 512), BF16)

    pltpu.make_async_copy(got.at[pl.ds(0, DEVICES - 1)], got.at[pl.ds(0, DEVICES - 1)], recv1).wait()
    for pair in range(3):
        both = got[:, pair * 16 : pair * 16 + 16, :].astype(F32)
        first, second = both[:, :8, :].reshape(256, 128), both[:, 8:, :].reshape(256, 128)
        vf[pair * 2, 0:256, :] = first
        if pair < 2:
            vf[pair * 2 + 1, 0:256, :] = second
        else:
            ninth[...] = second
    for j in range(5):
        vf[j, 256:288, :] = ninth[pl.ds(j, 32, stride=8), :]
        vb[0:288, j * 128 : j * 128 + 128] = vf[j].astype(BF16)

    edge_v = jnp.dot(vb[0:288, 0:512], gather_edge, preferred_element_type=F32)
    eo[...] = edge_v.astype(BF16)
    z_copies = []
    for n, other in enumerate((down, up)):
        copy = pltpu.make_async_remote_copy(
            src_ref=eo, dst_ref=ezi.at[n], send_sem=sendz.at[n], recv_sem=recvz.at[n],
            device_id=(me, other), device_id_type=MESH,
        )
        copy.start()
        z_copies.append(copy)

    wbuf[...] = jnp.dot(cc[:, 0:KPAD], vb[:, 0:512], preferred_element_type=F32)

    p0, p1 = iota((128, 128), 0), iota((128, 128), 1)
    dz, dy = (p0 // 8) % 8 - (p1 // 8) % 8, p0 % 8 - p1 % 8
    near = (p0 // 64 == p1 // 64) & (dz * dz + dy * dy == 1)
    near = jnp.where(near, 1.0, 0.0).astype(BF16)
    for j in range(4):
        total = jnp.dot(vb[0:288, j * 128 : j * 128 + 128], near, preferred_element_type=F32)
        total = total + x_sum(lambda n: vf[n], j)
        high, rest = split(total, 2)
        svb[0:288, j * 128 : j * 128 + 128] = high
        svb[KPAD : KPAD + 288, j * 128 : j * 128 + 128] = rest
    ubuf[...] = jnp.dot(cc[...], svb[...], preferred_element_type=F32)

    for copy in z_copies:
        copy.wait()
    lane288 = iota((288, 128), 1)
    beyond = jnp.where(lane288 < 64, ezi[0].astype(F32) * inside_up, ezi[1].astype(F32) * inside_down)
    vb[0:288, 640:768] = beyond.astype(BF16)
    hbuf[...] = jnp.dot(cc[:, 0:KPAD], vb[:, 512:768], preferred_element_type=F32)

    @pl.loop(0, ROWS // 16)
    def _(block):
        acc = [jnp.zeros((16, 128), F32) for _ in range(4)]
        mass = [jnp.zeros((16, 128), F32) for _ in range(4)]
        side = jnp.zeros((16, 128), F32)
        ends = jnp.zeros((16, 128), F32)
        for i in range(TERMS):
            at = pl.ds(pl.multiple_of(i * ROWS + block * 16, 16), 16)
            for j in range(4):
                k_row = kt[j * 16 + i : j * 16 + i + 1, :]
                w = wbuf[at, j * 128 : j * 128 + 128]
                acc[j] = acc[j] + ka[j, i : i + 1, :] * w - k_row * ubuf[at, j * 128 : j * 128 + 128]
                mass[j] = mass[j] + k_row * w
            side = side + hxc[i : i + 1, :] * hbuf[at, 0:128]
            ends = ends + hzc[i : i + 1, :] * hbuf[at, 128:256]
        here = pl.ds(pl.multiple_of(block * 16, 16), 16)
        for j in range(4):
            ra[j, here, :] = acc[j]
            bb[j, here, :] = mass[j]
        ex[here, :] = side
        ez[here, :] = ends

    end_parts = jnp.zeros((ROWS, 512), F32)
    for piece in reversed(split(ez[...], 2)):
        end_parts = end_parts + jnp.dot(piece, spread_edge, preferred_element_type=F32)
    lane = iota((ROWS, 128), 1)
    for j in range(4):
        total = ra[j] - x_sum(lambda n: bb[n], j) - yz_sum(bb[j]) - end_parts[:, j * 128 : j * 128 + 128]
        if j == 0:
            total = total - jnp.where(lane < 64, ex[...], 0.0)
        if j == 3:
            total = total - jnp.where(lane >= 64, ex[...], 0.0)
        total = 0.5 * total
        for c in range(CHIPS):
            ans[c * ANS + j * 8 : c * ANS + j * 8 + 8, :] = total[c * 8 : c * 8 + 8]
        ans[pl.ds(32 + j, CHIPS, stride=ANS), :] = total[128:ROWS]
    for j in range(4, 8):
        ans[pl.ds(32 + j, CHIPS, stride=ANS), :] = jnp.zeros((CHIPS, 128), F32)

    def block_of(c):
        return pl.ds(pl.multiple_of(c * ANS, 8), ANS)

    for ky, kx, kc in offsets:
        if kc == 0:
            target = chip_at(ky, kx)
            pltpu.make_async_remote_copy(
                src_ref=ans.at[block_of(target), :], dst_ref=ret.at[block_of(chip), :], send_sem=send2, recv_sem=recv2,
                device_id=(target * 2 + core, zi), device_id_type=MESH,
            ).start()
    ret[block_of(chip), :] = ans[block_of(chip), :]
    rest = ret.at[pl.ds(0, (CHIPS - 1) * ANS), :]
    pltpu.make_async_copy(rest, rest, recv2).wait()

    low16 = iota((CHIPS, 128), 1) < 64
    for first in range(0, OWN, 2):
        second = min(first + 1, OWN - 1)
        for j in range(4):
            one = ret[pl.ds(j * 8 + first if first < 8 else 32 + j, CHIPS, stride=ANS), :]
            two = ret[pl.ds(j * 8 + second if second < 8 else 32 + j, CHIPS, stride=ANS), :]
            turn[pl.ds(j, CHIPS, stride=8), :] = jnp.where(low16, one, pltpu.roll(two, 64, 1))
            turn[pl.ds(4 + j, CHIPS, stride=8), :] = jnp.where(low16, pltpu.roll(one, 64, 1), two)
        turned = turn[...].T
        o_ref[first] = turned[:64].reshape(8, 8, 128)
        if second > first:
            o_ref[second] = turned[64:].reshape(8, 8, 128)

    pltpu.make_async_copy(got.at[pl.ds(0, DEVICES - 1)], got.at[pl.ds(0, DEVICES - 1)], send1).wait()
    pltpu.make_async_copy(rest, rest, send2).wait()


def body(mode_field, kl_coeff, mode_slot, trip_kl, trip_in, trip_out, trip_weight):
    vmem = pl.BlockSpec(memory_space=pltpu.VMEM)
    dma = pltpu.SemaphoreType.DMA
    call = pl.pallas_call(
        kernel,
        out_shape=jax.ShapeDtypeStruct(mode_field.shape, F32),
        in_specs=[vmem] * 7,
        out_specs=vmem,
        scratch_shapes=[
            pltpu.VMEM((CHIPS * 64, 128), F32),
            pltpu.VMEM((CHIPS, MSG, 128), BF16),
            pltpu.VMEM((DEVICES, MSG, 128), BF16),
            pltpu.VMEM((256, 128), F32),
            pltpu.VMEM((5, 288, 128), F32),
            pltpu.VMEM((KPAD, 768), BF16),
            pltpu.VMEM((2 * KPAD, 512), BF16),
            pltpu.VMEM((TERMS * ROWS, TRIPS_PAD), BF16),
            pltpu.VMEM((TERMS * ROWS, 2 * KPAD), BF16),
            pltpu.VMEM((TERMS * ROWS, 512), F32),
            pltpu.VMEM((TERMS * ROWS, 512), F32),
            pltpu.VMEM((TERMS * ROWS, 256), F32),
            pltpu.VMEM((128, 128), F32),
            pltpu.VMEM((4, 16, 128), F32),
            pltpu.VMEM((16, 128), F32),
            pltpu.VMEM((2, 16, 128), F32),
            pltpu.VMEM((16, 128), F32),
            pltpu.VMEM((16, 128), F32),
            pltpu.VMEM((288, 128), BF16),
            pltpu.VMEM((2, 288, 128), BF16),
            pltpu.VMEM((4, ROWS, 128), F32),
            pltpu.VMEM((4, ROWS, 128), F32),
            pltpu.VMEM((ROWS, 128), F32),
            pltpu.VMEM((ROWS, 128), F32),
            pltpu.VMEM((CHIPS * ANS, 128), F32),
            pltpu.VMEM((CHIPS * ANS, 128), F32),
            pltpu.VMEM((128, 128), F32),
            pltpu.VMEM((16, KPAD), F32),
            pltpu.VMEM((8, TRIPS_PAD), jnp.int32),
            pltpu.VMEM((8, TRIPS_PAD), F32),
            dma, dma, dma((2,)), dma((2,)), dma((2,)), dma((2,)), dma, dma,
        ],
        compiler_params=pltpu.CompilerParams(
            collective_id=0, has_side_effects=True, vmem_limit_bytes=48 << 20
        ),
    )
    return call(
        mode_field, kl_coeff, mode_slot[None, :], trip_kl[None, :], trip_in[None, :], trip_out[None, :],
        trip_weight[None, :],
    )


def solution(mesh):
    placed = (P("mode", "space", None, None), P(None, "space", None, None), P(), P(), P(), P(), P())
    return jax.shard_map(
        body, mesh=mesh, in_specs=placed, out_specs=P("mode", "space", None, None), check_vma=False
    )
```

```python
import jax
import jax.numpy as jnp
from jax import lax
from jax.experimental import pallas as pl
from jax.experimental.pallas import tpu as pltpu
from jax.sharding import PartitionSpec as P

MESH = pl.DeviceIdType.MESH
F32 = jnp.float32
BF16 = jnp.bfloat16
NT = (((1,), (1,)), ((), ()))

SIDE = 4
CHIPS = 16
OWN = 9
TERMS = 11
TRIPS = 1606
TRIPS_PAD = 1664
MODES = 286
ROWS = 144
KPAD = 384
MSG = 48
ANS = 40


def iota(shape, dim):
    return lax.broadcasted_iota(jnp.int32, shape, dim)


def lane_of(value):
    return iota(value.shape, value.ndim - 1)


def split(value, parts):
    out = []
    for _ in range(parts):
        piece = value.astype(BF16)
        out.append(piece)
        value = value - piece.astype(F32)
    return out


def yz_sum(value):
    lane = lane_of(value)
    y = lane % 8
    z = (lane // 8) % 8
    total = jnp.where(y > 0, pltpu.roll(value, 1, 1), 0.0)
    total = total + jnp.where(y < 7, pltpu.roll(value, 127, 1), 0.0)
    total = total + jnp.where(z > 0, pltpu.roll(value, 8, 1), 0.0)
    return total + jnp.where(z < 7, pltpu.roll(value, 120, 1), 0.0)


def x_sum(tiles, j):
    lane = lane_of(tiles(0))
    left = tiles(j - 1) if j > 0 else jnp.where(lane >= 64, pltpu.roll(tiles(3), 64, 1), 0.0)
    right = tiles(j + 1) if j < 3 else jnp.where(lane < 64, pltpu.roll(tiles(0), 64, 1), 0.0)
    return left + right


def column_select(rows, chip, half, j):
    target = 8 * chip + j + 4 * half
    target = jnp.where(j == 4, jnp.where(half == 0, 8 * chip - 1, 8 * chip + 8), target)
    target = jnp.where(j > 4, -1, target)
    return jnp.where(iota((rows, 128), 1) == target, 1.0, 0.0).astype(BF16)


def edge_gather():
    row = iota((512, 128), 0)
    out = iota((512, 128), 1)
    j, half, z, y = row // 128, (row // 64) % 2, (row // 8) % 8, row % 8
    place = (j + 4 * half) * 8 + y
    hit = ((z == 0) & (out == place)) | ((z == 7) & (out == 64 + place))
    return jnp.where(hit, 1.0, 0.0).astype(BF16)


def edge_spread():
    out = iota((128, 512), 1)
    row = iota((128, 512), 0)
    j, half, z, y = out // 128, (out // 64) % 2, (out // 8) % 8, out % 8
    place = (j + 4 * half) * 8 + y
    hit = ((z == 7) & (row == place)) | ((z == 0) & (row == 64 + place))
    return jnp.where(hit, 1.0, 0.0).astype(BF16)


def kernel(
    v_hbm, k_hbm, slot_hbm, kl_hbm, in_hbm, out_hbm, w_hbm, o_ref,
    v_ref, k_ref, slot_ref, kl_ref, in_ref, out_ref, w_ref,
    pack, msg, got, ninth, vf, vb, svb, onehot, cc, wbuf, ubuf, hbuf, main,
    kt, ka, eok, kzi, hxc, hzc, eo, ezi, ra, bb, ex, ez, ans, ret, turn, places, trip, table,
    load, send1, recv1, sendr, recvr, sendk, recvk, sendz, recvz, send2, recv2,
):
    loads = [
        pltpu.make_async_copy(src, dst, load.at[n])
        for n, (src, dst) in enumerate((
            (v_hbm, v_ref), (in_hbm, in_ref), (out_hbm, out_ref), (kl_hbm, kl_ref), (slot_hbm, slot_ref),
            (w_hbm, w_ref), (k_hbm, k_ref),
        ))
    ]
    loads[0].start()

    me = lax.axis_index("mode")
    zi = lax.axis_index("space")
    nz = lax.axis_size("space")
    chip, core = me // 2, me % 2
    ypos, xpos = chip // SIDE, chip % SIDE

    offsets = [(ky, kx) for ky in range(SIDE) for kx in range(SIDE) if (ky, kx) != (0, 0)]
    offsets.sort(key=lambda o: -(min(o[0], SIDE - o[0]) + min(o[1], SIDE - o[1])))

    def chip_at(ky, kx):
        return lax.rem(ypos + ky, SIDE) * SIDE + lax.rem(xpos + kx, SIDE)

    up, down = lax.rem(zi + 1, nz), lax.rem(zi + nz - 1, nz)

    barrier = pltpu.get_barrier_semaphore()
    twin = chip * 2 + 1 - core
    around = [(n, who, other) for n, other in enumerate((down, up)) for who in (me, twin)]
    for ky, kx in offsets:
        pl.semaphore_signal(barrier, inc=1, device_id=(chip_at(ky, kx) * 2 + core, zi), device_id_type=MESH)
    pl.semaphore_signal(barrier, inc=1, device_id=(twin, zi), device_id_type=MESH)
    for _, who, other in around:
        pl.semaphore_signal(barrier, inc=1, device_id=(who, other), device_id_type=MESH)

    for copy in loads[1:]:
        copy.start()

    row = iota((256, 128), 0)
    select = column_select(256, (row % 128) // 8, row // 128, row % 8)
    low = iota((128, 128), 1) < 64
    loads[0].wait()
    for m in range(OWN):
        field = v_ref[m].astype(F32).reshape(64, 128)
        field = jnp.concatenate([field, field], axis=0).astype(BF16)
        turned = lax.dot_general(select, field, NT, preferred_element_type=F32)
        turned = jnp.where(low, turned[:128], turned[128:])
        for c in range(CHIPS):
            if m < 8:
                pack[pl.ds(c * 64 + m, 8, stride=8), :] = turned[c * 8 : c * 8 + 8]
            else:
                pack[pl.ds(c * 64 + 40, 8), :] = turned[c * 8 : c * 8 + 8]
    for c in range(CHIPS):
        msg[c] = pack[pl.ds(c * 64, MSG), :].astype(BF16)
    got[core, 0] = msg[chip]

    pl.semaphore_wait(barrier, len(offsets) + 1 + len(around))
    for ky, kx in offsets:
        target = chip_at(ky, kx)
        pltpu.make_async_remote_copy(
            src_ref=msg.at[target], dst_ref=got.at[core, ky * SIDE + kx], send_sem=send1, recv_sem=recv1.at[ky],
            device_id=(target * 2 + core, zi), device_id_type=MESH,
        ).start()

    gather_edge = edge_gather()
    spread_edge = edge_spread()
    kt[...] = jnp.zeros_like(kt)
    row16 = iota((16, 128), 0)
    select_k = column_select(16, chip, row16 // 8, row16 % 8)
    loads[6].wait()
    for i in range(TERMS):
        block = k_ref[i].reshape(64, 128)
        block = jnp.concatenate([block, block], axis=0)
        turned = jnp.zeros((16, 128), F32)
        for piece in reversed(split(block, 3)):
            turned = turned + lax.dot_general(select_k, piece, NT, preferred_element_type=F32)
        kt[pl.ds(i, 8, stride=16), :] = jnp.where(low[:8], turned[:8], turned[8:])

    def k_tile(j):
        return kt[j * 16 : j * 16 + 16, :]

    whole = jnp.concatenate([k_tile(j) for j in range(4)], axis=1)
    edge = jnp.zeros((16, 128), F32)
    for piece in reversed(split(whole, 3)):
        edge = edge + jnp.dot(piece, gather_edge, preferred_element_type=F32)
    eok[...] = edge
    k_copies = []
    for n, other in enumerate((down, up)):
        copy = pltpu.make_async_remote_copy(
            src_ref=eok, dst_ref=kzi.at[n], send_sem=sendk.at[n], recv_sem=recvk.at[n],
            device_id=(me, other), device_id_type=MESH,
        )
        copy.start()
        k_copies.append(copy)

    for copy in loads[1:6]:
        copy.wait()
    trip[...] = jnp.full(trip.shape, -1, jnp.int32)
    trip[0:1, 0:TRIPS] = in_ref[...].reshape(1, TRIPS)
    trip[1:2, 0:TRIPS] = out_ref[...].reshape(1, TRIPS)
    trip[2:3, 0:TRIPS] = kl_ref[...].reshape(1, TRIPS)
    table[...] = jnp.zeros(table.shape, F32)
    table[0:1, 0:TRIPS] = w_ref[...].astype(F32).reshape(1, TRIPS)
    slots = jnp.broadcast_to(slot_ref[...].reshape(1, MODES), (16, MODES))
    dev = lax.shift_right_logical(slots * 57, 9)
    kind = slots - dev * OWN
    away_y = (ypos - dev // 8 + SIDE) % SIDE
    away_x = (xpos - (dev // 2) % SIDE + SIDE) % SIDE
    came = (dev % 2) * CHIPS + away_y * SIDE + away_x
    column = jnp.where(kind < 8, came * 8 + kind, 256 + came)
    place = jnp.where(kind < 8, (dev // 2) * 8 + kind, 128 + dev // 2)
    place = jnp.where(dev % 2 == core, place, 240)
    row16m = iota((16, MODES), 0)
    number = jnp.where(row16m < 2, column, place)
    digits = jnp.where(row16m % 2 == 0, lax.shift_right_logical(number, 4), number & 15)
    digits = jnp.where(row16m < 4, digits, 0).astype(F32)
    places[...] = jnp.zeros((16, KPAD), F32)
    places[:, 0:MODES] = digits
    digits = places[...].astype(BF16)
    mode_row = iota((KPAD, TRIPS_PAD), 0)
    hit_in = jnp.where(mode_row == trip[0:1, :], 1.0, 0.0).astype(BF16)
    look_in = jnp.dot(digits, hit_in, preferred_element_type=F32)
    hit_out = jnp.where(mode_row == trip[1:2, :], 1.0, 0.0).astype(BF16)
    look_out = jnp.dot(digits, hit_out, preferred_element_type=F32)
    look_in = look_in.T
    column_t = look_in[:, 0:1] * 16.0 + look_in[:, 1:2]
    place_t = (look_out[2:3] * 16.0 + look_out[3:4]).astype(jnp.int32)
    key_t = jnp.where(place_t < ROWS, trip[2:3, :] * ROWS + place_t, -1)
    trip[3:4, :] = key_t
    lane_number = iota((TRIPS_PAD, KPAD), 1).astype(F32)
    by_column = jnp.where(lane_number == column_t, 1.0, 0.0).astype(BF16)

    @pl.loop(0, TERMS)
    def _(i):
        rows = iota((ROWS, TRIPS_PAD), 0) + i * ROWS
        part = jnp.where(rows == trip[3:4, :], table[0:1, :], 0.0).astype(BF16)
        onehot[pl.ds(pl.multiple_of(i * ROWS, 16), ROWS), :] = part

    coupling = jnp.dot(onehot[...], by_column, preferred_element_type=F32).astype(BF16)
    cc[:, 0:KPAD] = coupling
    cc[:, KPAD:] = coupling

    for copy in k_copies:
        copy.wait()
    lane16 = iota((16, 128), 1)
    inside_up = jnp.where(zi < nz - 1, 1.0, 0.0)
    inside_down = jnp.where(zi > 0, 1.0, 0.0)
    k_beyond = jnp.where(lane16 < 64, kzi[0] * inside_up, kzi[1] * inside_down)
    hzc[...] = pltpu.roll(edge, 64, 1) + k_beyond
    hxc[...] = jnp.where(lane16 < 64, k_tile(0), k_tile(3)) + k_tile(4)
    spread = jnp.zeros((16, 512), F32)
    for piece in reversed(split(k_beyond, 3)):
        spread = spread + jnp.dot(piece, spread_edge, preferred_element_type=F32)
    for j in range(4):
        total = 6.0 * k_tile(j) + x_sum(k_tile, j) + yz_sum(k_tile(j)) + spread[:, j * 128 : j * 128 + 128]
        if j == 0:
            total = total + jnp.where(lane16 < 64, k_tile(4), 0.0)
        if j == 3:
            total = total + jnp.where(lane16 >= 64, k_tile(4), 0.0)
        ka[j] = total

    vb[288:KPAD, :] = jnp.zeros((KPAD - 288, 768), BF16)
    svb[288:KPAD, :] = jnp.zeros((KPAD - 288, 512), BF16)
    svb[KPAD + 288 :, :] = jnp.zeros((KPAD - 288, 512), BF16)

    relays = []
    for ky in (0, 1, 3, 2):
        first = 1 if ky == 0 else 0
        here = got.at[core, pl.ds(ky * SIDE + first, SIDE - first)]
        pltpu.make_async_copy(here, here, recv1.at[ky]).wait()
        line = got.at[core, pl.ds(ky * SIDE, SIDE)]
        copy = pltpu.make_async_remote_copy(
            src_ref=line, dst_ref=line, send_sem=sendr.at[ky], recv_sem=recvr.at[ky],
            device_id=(twin, zi), device_id_type=MESH,
        )
        copy.start()
        relays.append(copy)

    def unpack(half):
        most = pl.ds(pl.multiple_of(half * 128, 128), 128)
        rest = pl.ds(pl.multiple_of(256 + half * 16, 16), 16)
        for pair in range(3):
            both = got[half, :, pair * 16 : pair * 16 + 16, :].astype(F32)
            vf[pair * 2, most, :] = both[:, :8, :].reshape(128, 128)
            if pair < 2:
                vf[pair * 2 + 1, most, :] = both[:, 8:, :].reshape(128, 128)
            else:
                ninth[...] = both[:, 8:, :].reshape(128, 128)
        for j in range(5):
            vf[j, rest, :] = ninth[pl.ds(j, 16, stride=8), :]
            vb[most, j * 128 : j * 128 + 128] = vf[j, most, :].astype(BF16)
            vb[rest, j * 128 : j * 128 + 128] = vf[j, rest, :].astype(BF16)
        return most, rest

    most, rest = unpack(core)
    edges = jnp.concatenate(
        [
            jnp.dot(vb[most, 0:512], gather_edge, preferred_element_type=F32),
            jnp.dot(vb[rest, 0:512], gather_edge, preferred_element_type=F32),
            jnp.zeros((16, 128), F32),
        ],
        axis=0,
    )
    low80 = iota((80, 128), 1) < 64
    eo[0] = jnp.where(low80, edges[:80], pltpu.roll(edges[80:], 64, 1)).astype(BF16)
    eo[1] = jnp.where(low80, pltpu.roll(edges[:80], 64, 1), edges[80:]).astype(BF16)
    z_copies = []
    for n, who, other in around:
        cross = 0 if who is me else 1
        copy = pltpu.make_async_remote_copy(
            src_ref=eo.at[n], dst_ref=ezi.at[n, core], send_sem=sendz.at[n, cross], recv_sem=recvz.at[n, cross],
            device_id=(who, other), device_id_type=MESH,
        )
        copy.start()
        z_copies.append(copy)
    for copy in relays:
        copy.wait()
    unpack(1 - core)

    wbuf[...] = jnp.dot(cc[:, 0:KPAD], vb[:, 0:640], preferred_element_type=F32)

    p0, p1 = iota((128, 128), 0), iota((128, 128), 1)
    dz, dy = (p0 // 8) % 8 - (p1 // 8) % 8, p0 % 8 - p1 % 8
    near = (p0 // 64 == p1 // 64) & (dz * dz + dy * dy == 1)
    near = jnp.where(near, 1.0, 0.0).astype(BF16)
    for j in range(4):
        total = jnp.dot(vb[0:288, j * 128 : j * 128 + 128], near, preferred_element_type=F32)
        total = total + x_sum(lambda n: vf[n], j)
        high, rest = split(total, 2)
        svb[0:288, j * 128 : j * 128 + 128] = high
        svb[KPAD : KPAD + 288, j * 128 : j * 128 + 128] = rest
    ubuf[...] = jnp.dot(cc[...], svb[...], preferred_element_type=F32)

    @pl.loop(0, ROWS // 16)
    def _(block):
        acc = [jnp.zeros((16, 128), F32) for _ in range(4)]
        mass = [jnp.zeros((16, 128), F32) for _ in range(4)]
        side = jnp.zeros((16, 128), F32)
        for i in range(TERMS):
            at = pl.ds(pl.multiple_of(i * ROWS + block * 16, 16), 16)
            for j in range(4):
                k_row = kt[j * 16 + i : j * 16 + i + 1, :]
                w = wbuf[at, j * 128 : j * 128 + 128]
                acc[j] = acc[j] + ka[j, i : i + 1, :] * w - k_row * ubuf[at, j * 128 : j * 128 + 128]
                mass[j] = mass[j] + k_row * w
            side = side + hxc[i : i + 1, :] * wbuf[at, 512:640]
        here = pl.ds(pl.multiple_of(block * 16, 16), 16)
        for j in range(4):
            ra[j, here, :] = acc[j]
            bb[j, here, :] = mass[j]
        ex[here, :] = side

    lane = iota((ROWS, 128), 1)
    for j in range(4):
        total = ra[j] - x_sum(lambda n: bb[n], j) - yz_sum(bb[j])
        if j == 0:
            total = total - jnp.where(lane < 64, ex[...], 0.0)
        if j == 3:
            total = total - jnp.where(lane >= 64, ex[...], 0.0)
        main[j] = total

    for copy in z_copies:
        copy.wait()
    for half in range(2):
        above = ezi[0, half].astype(F32) * inside_up
        below = ezi[1, half].astype(F32) * inside_down
        one = jnp.where(low80, above, pltpu.roll(below, 64, 1)).astype(BF16)
        two = jnp.where(low80, pltpu.roll(above, 64, 1), below).astype(BF16)
        vb[half * 128 : half * 128 + 80, 640:768] = one
        vb[half * 128 + 80 : half * 128 + 128, 640:768] = two[:48]
        vb[256 + half * 16 : 272 + half * 16, 640:768] = two[48:64]
    hbuf[...] = jnp.dot(cc[:, 0:KPAD], vb[:, 640:768], preferred_element_type=F32)

    @pl.loop(0, ROWS // 16)
    def _(block):
        ends = jnp.zeros((16, 128), F32)
        for i in range(TERMS):
            at = pl.ds(pl.multiple_of(i * ROWS + block * 16, 16), 16)
            ends = ends + hzc[i : i + 1, :] * hbuf[at, :]
        ez[pl.ds(pl.multiple_of(block * 16, 16), 16), :] = ends

    end_parts = jnp.zeros((ROWS, 512), F32)
    for piece in reversed(split(ez[...], 2)):
        end_parts = end_parts + jnp.dot(piece, spread_edge, preferred_element_type=F32)
    for j in range(4):
        total = main[j] - end_parts[:, j * 128 : j * 128 + 128]
        total = 0.5 * total
        for c in range(CHIPS):
            ans[c * ANS + j * 8 : c * ANS + j * 8 + 8, :] = total[c * 8 : c * 8 + 8]
        ans[pl.ds(32 + j, CHIPS, stride=ANS), :] = total[128:ROWS]
    for j in range(4, 8):
        ans[pl.ds(32 + j, CHIPS, stride=ANS), :] = jnp.zeros((CHIPS, 128), F32)

    def block_of(c):
        return pl.ds(pl.multiple_of(c * ANS, 8), ANS)

    for ky, kx in offsets:
        target = chip_at(ky, kx)
        pltpu.make_async_remote_copy(
            src_ref=ans.at[block_of(target), :], dst_ref=ret.at[block_of(chip), :], send_sem=send2, recv_sem=recv2,
            device_id=(target * 2 + core, zi), device_id_type=MESH,
        ).start()
    ret[block_of(chip), :] = ans[block_of(chip), :]
    rest = ret.at[pl.ds(0, (CHIPS - 1) * ANS), :]
    pltpu.make_async_copy(rest, rest, recv2).wait()

    low16 = iota((CHIPS, 128), 1) < 64
    for first in range(0, OWN, 2):
        second = min(first + 1, OWN - 1)
        for j in range(4):
            one = ret[pl.ds(j * 8 + first if first < 8 else 32 + j, CHIPS, stride=ANS), :]
            two = ret[pl.ds(j * 8 + second if second < 8 else 32 + j, CHIPS, stride=ANS), :]
            turn[pl.ds(j, CHIPS, stride=8), :] = jnp.where(low16, one, pltpu.roll(two, 64, 1))
            turn[pl.ds(4 + j, CHIPS, stride=8), :] = jnp.where(low16, pltpu.roll(one, 64, 1), two)
        turned = turn[...].T
        o_ref[first] = turned[:64].reshape(8, 8, 128)
        if second > first:
            o_ref[second] = turned[64:].reshape(8, 8, 128)

    sent = msg.at[pl.ds(0, CHIPS - 1)]
    pltpu.make_async_copy(sent, sent, send1).wait()
    pltpu.make_async_copy(rest, rest, send2).wait()


def body(mode_field, kl_coeff, mode_slot, trip_kl, trip_in, trip_out, trip_weight):
    vmem = pl.BlockSpec(memory_space=pltpu.VMEM)
    operands = (mode_field, kl_coeff, mode_slot, trip_kl, trip_in, trip_out, trip_weight)
    dma = pltpu.SemaphoreType.DMA
    call = pl.pallas_call(
        kernel,
        out_shape=jax.ShapeDtypeStruct(mode_field.shape, F32),
        in_specs=[pl.BlockSpec(memory_space=pltpu.HBM)] * 7,
        out_specs=vmem,
        scratch_shapes=[
            *(pltpu.VMEM(a.shape, a.dtype) for a in operands),
            pltpu.VMEM((CHIPS * 64, 128), F32),
            pltpu.VMEM((CHIPS, MSG, 128), BF16),
            pltpu.VMEM((2, CHIPS, MSG, 128), BF16),
            pltpu.VMEM((128, 128), F32),
            pltpu.VMEM((5, 288, 128), F32),
            pltpu.VMEM((KPAD, 768), BF16),
            pltpu.VMEM((2 * KPAD, 512), BF16),
            pltpu.VMEM((TERMS * ROWS, TRIPS_PAD), BF16),
            pltpu.VMEM((TERMS * ROWS, 2 * KPAD), BF16),
            pltpu.VMEM((TERMS * ROWS, 640), F32),
            pltpu.VMEM((TERMS * ROWS, 512), F32),
            pltpu.VMEM((TERMS * ROWS, 128), F32),
            pltpu.VMEM((4, ROWS, 128), F32),
            pltpu.VMEM((128, 128), F32),
            pltpu.VMEM((4, 16, 128), F32),
            pltpu.VMEM((16, 128), F32),
            pltpu.VMEM((2, 16, 128), F32),
            pltpu.VMEM((16, 128), F32),
            pltpu.VMEM((16, 128), F32),
            pltpu.VMEM((2, 80, 128), BF16),
            pltpu.VMEM((2, 2, 80, 128), BF16),
            pltpu.VMEM((4, ROWS, 128), F32),
            pltpu.VMEM((4, ROWS, 128), F32),
            pltpu.VMEM((ROWS, 128), F32),
            pltpu.VMEM((ROWS, 128), F32),
            pltpu.VMEM((CHIPS * ANS, 128), F32),
            pltpu.VMEM((CHIPS * ANS, 128), F32),
            pltpu.VMEM((128, 128), F32),
            pltpu.VMEM((16, KPAD), F32),
            pltpu.VMEM((8, TRIPS_PAD), jnp.int32),
            pltpu.VMEM((8, TRIPS_PAD), F32),
            dma((7,)), dma, dma((SIDE,)), dma((SIDE,)), dma((SIDE,)), dma((2,)), dma((2,)), dma((2, 2)), dma((2, 2)), dma, dma,
        ],
        compiler_params=pltpu.CompilerParams(
            collective_id=0, has_side_effects=True, vmem_limit_bytes=40 << 20
        ),
    )
    return call(*(pltpu.with_memory_space_constraint(a, pltpu.HBM) for a in operands))


def solution(mesh):
    placed = (P("mode", "space", None, None), P(None, "space", None, None), P(), P(), P(), P(), P())
    return jax.shard_map(
        body, mesh=mesh, in_specs=placed, out_specs=P("mode", "space", None, None), check_vma=False
    )
```

```python
import jax
import jax.numpy as jnp
from jax import lax
from jax.experimental import pallas as pl
from jax.experimental.pallas import tpu as pltpu
from jax.sharding import PartitionSpec as P

MESH = pl.DeviceIdType.MESH
F32 = jnp.float32
BF16 = jnp.bfloat16
NT = (((1,), (1,)), ((), ()))

SIDE = 4
CHIPS = 16
OWN = 9
TERMS = 11
TRIPS = 1606
TRIPS_PAD = 1664
MODES = 286
ROWS = 144
KPAD = 384
MSG = 48
ANS = 40


def iota(shape, dim):
    return lax.broadcasted_iota(jnp.int32, shape, dim)


def lane_of(value):
    return iota(value.shape, value.ndim - 1)


def split(value, parts):
    out = []
    for _ in range(parts):
        piece = value.astype(BF16)
        out.append(piece)
        value = value - piece.astype(F32)
    return out


def yz_sum(value):
    lane = lane_of(value)
    y = lane % 8
    z = (lane // 8) % 8
    total = jnp.where(y > 0, pltpu.roll(value, 1, 1), 0.0)
    total = total + jnp.where(y < 7, pltpu.roll(value, 127, 1), 0.0)
    total = total + jnp.where(z > 0, pltpu.roll(value, 8, 1), 0.0)
    return total + jnp.where(z < 7, pltpu.roll(value, 120, 1), 0.0)


def x_sum(tiles, j):
    lane = lane_of(tiles(0))
    left = tiles(j - 1) if j > 0 else jnp.where(lane >= 64, pltpu.roll(tiles(3), 64, 1), 0.0)
    right = tiles(j + 1) if j < 3 else jnp.where(lane < 64, pltpu.roll(tiles(0), 64, 1), 0.0)
    return left + right


def column_select(rows, chip, half, j):
    target = 8 * chip + j + 4 * half
    target = jnp.where(j == 4, jnp.where(half == 0, 8 * chip - 1, 8 * chip + 8), target)
    target = jnp.where(j > 4, -1, target)
    return jnp.where(iota((rows, 128), 1) == target, 1.0, 0.0).astype(BF16)


def edge_gather():
    row = iota((512, 128), 0)
    out = iota((512, 128), 1)
    j, half, z, y = row // 128, (row // 64) % 2, (row // 8) % 8, row % 8
    place = (j + 4 * half) * 8 + y
    hit = ((z == 0) & (out == place)) | ((z == 7) & (out == 64 + place))
    return jnp.where(hit, 1.0, 0.0).astype(BF16)


def edge_spread():
    out = iota((128, 512), 1)
    row = iota((128, 512), 0)
    j, half, z, y = out // 128, (out // 64) % 2, (out // 8) % 8, out % 8
    place = (j + 4 * half) * 8 + y
    hit = ((z == 7) & (row == place)) | ((z == 0) & (row == 64 + place))
    return jnp.where(hit, 1.0, 0.0).astype(BF16)


def kernel(
    v_hbm, k_hbm, slot_hbm, kl_hbm, in_hbm, out_hbm, w_hbm, o_ref,
    v_ref, k_ref, slot_ref, kl_ref, in_ref, out_ref, w_ref,
    pack, msg, got, ninth, vf, vb, svb, onehot, cc, wbuf, ubuf, hbuf, main,
    kt, ka, eok, kzi, hxc, hzc, eo, ezi, ra, bb, ex, ez, ans, ret, turn, places, trip, table,
    load, ready, send1, recv1, sendr, recvr, sendk, recvk, sendz, recvz, send2, recv2,
):
    loads = [
        pltpu.make_async_copy(src, dst, load.at[n])
        for n, (src, dst) in enumerate((
            (v_hbm, v_ref), (in_hbm, in_ref), (out_hbm, out_ref), (kl_hbm, kl_ref), (slot_hbm, slot_ref),
            (w_hbm, w_ref), (k_hbm, k_ref),
        ))
    ]
    loads[0].start()

    me = lax.axis_index("mode")
    zi = lax.axis_index("space")
    nz = lax.axis_size("space")
    chip, core = me // 2, me % 2
    ypos, xpos = chip // SIDE, chip % SIDE

    offsets = [(ky, kx) for ky in range(SIDE) for kx in range(SIDE) if (ky, kx) != (0, 0)]
    offsets.sort(key=lambda o: -(min(o[0], SIDE - o[0]) + min(o[1], SIDE - o[1])))

    def chip_at(ky, kx):
        return lax.rem(ypos + ky, SIDE) * SIDE + lax.rem(xpos + kx, SIDE)

    up, down = lax.rem(zi + 1, nz), lax.rem(zi + nz - 1, nz)

    barrier = pltpu.get_barrier_semaphore()
    twin = chip * 2 + 1 - core
    around = [(n, who, other) for n, other in enumerate((down, up)) for who in (me, twin)]
    for ky, kx in offsets:
        pl.semaphore_signal(barrier, inc=1, device_id=(chip_at(ky, kx) * 2 + core, zi), device_id_type=MESH)
    pl.semaphore_signal(barrier, inc=1, device_id=(twin, zi), device_id_type=MESH)

    odd = lax.rem(zi, 2)

    @pl.when(odd == 0)
    def _():
        for _, who, other in around:
            pl.semaphore_signal(barrier, inc=1, device_id=(who, other), device_id_type=MESH)

    for copy in loads[1:]:
        copy.start()

    row = iota((256, 128), 0)
    select = column_select(256, (row % 128) // 8, row // 128, row % 8)
    low = iota((128, 128), 1) < 64
    loads[0].wait()
    for m in range(OWN):
        field = v_ref[m].astype(F32).reshape(64, 128)
        field = jnp.concatenate([field, field], axis=0).astype(BF16)
        turned = lax.dot_general(select, field, NT, preferred_element_type=F32)
        turned = jnp.where(low, turned[:128], turned[128:])
        for c in range(CHIPS):
            if m < 8:
                pack[pl.ds(c * 64 + m, 8, stride=8), :] = turned[c * 8 : c * 8 + 8]
            else:
                pack[pl.ds(c * 64 + 40, 8), :] = turned[c * 8 : c * 8 + 8]
    for c in range(CHIPS):
        msg[c] = pack[pl.ds(c * 64, MSG), :].astype(BF16)
    got[core, 0] = msg[chip]

    pl.semaphore_wait(barrier, len(offsets) + 1 + len(around) * odd)

    @pl.when(odd == 1)
    def _():
        for _, who, other in around:
            pl.semaphore_signal(ready, inc=1, device_id=(who, other), device_id_type=MESH)

    for ky, kx in offsets:
        target = chip_at(ky, kx)
        pltpu.make_async_remote_copy(
            src_ref=msg.at[target], dst_ref=got.at[core, ky * SIDE + kx], send_sem=send1, recv_sem=recv1.at[ky],
            device_id=(target * 2 + core, zi), device_id_type=MESH,
        ).start()

    gather_edge = edge_gather()
    spread_edge = edge_spread()
    kt[...] = jnp.zeros_like(kt)
    row16 = iota((16, 128), 0)
    select_k = column_select(16, chip, row16 // 8, row16 % 8)
    loads[6].wait()
    for i in range(TERMS):
        block = k_ref[i].reshape(64, 128)
        block = jnp.concatenate([block, block], axis=0)
        turned = jnp.zeros((16, 128), F32)
        for piece in reversed(split(block, 3)):
            turned = turned + lax.dot_general(select_k, piece, NT, preferred_element_type=F32)
        kt[pl.ds(i, 8, stride=16), :] = jnp.where(low[:8], turned[:8], turned[8:])

    def k_tile(j):
        return kt[j * 16 : j * 16 + 16, :]

    whole = jnp.concatenate([k_tile(j) for j in range(4)], axis=1)
    edge = jnp.zeros((16, 128), F32)
    for piece in reversed(split(whole, 3)):
        edge = edge + jnp.dot(piece, gather_edge, preferred_element_type=F32)
    eok[...] = edge
    k_copies = []
    for n, other in enumerate((down, up)):
        copy = pltpu.make_async_remote_copy(
            src_ref=eok, dst_ref=kzi.at[n], send_sem=sendk.at[n], recv_sem=recvk.at[n],
            device_id=(me, other), device_id_type=MESH,
        )
        k_copies.append(copy)

    @pl.when(odd == 1)
    def _():
        for copy in k_copies:
            copy.start()


    for copy in loads[1:6]:
        copy.wait()
    trip[...] = jnp.full(trip.shape, -1, jnp.int32)
    trip[0:1, 0:TRIPS] = in_ref[...].reshape(1, TRIPS)
    trip[1:2, 0:TRIPS] = out_ref[...].reshape(1, TRIPS)
    trip[2:3, 0:TRIPS] = kl_ref[...].reshape(1, TRIPS)
    table[...] = jnp.zeros(table.shape, F32)
    table[0:1, 0:TRIPS] = w_ref[...].astype(F32).reshape(1, TRIPS)
    slots = jnp.broadcast_to(slot_ref[...].reshape(1, MODES), (16, MODES))
    dev = lax.shift_right_logical(slots * 57, 9)
    kind = slots - dev * OWN
    away_y = (ypos - dev // 8 + SIDE) % SIDE
    away_x = (xpos - (dev // 2) % SIDE + SIDE) % SIDE
    came = (dev % 2) * CHIPS + away_y * SIDE + away_x
    column = jnp.where(kind < 8, came * 8 + kind, 256 + came)
    place = jnp.where(kind < 8, (dev // 2) * 8 + kind, 128 + dev // 2)
    place = jnp.where(dev % 2 == core, place, 240)
    row16m = iota((16, MODES), 0)
    number = jnp.where(row16m < 2, column, place)
    digits = jnp.where(row16m % 2 == 0, lax.shift_right_logical(number, 4), number & 15)
    digits = jnp.where(row16m < 4, digits, 0).astype(F32)
    places[...] = jnp.zeros((16, KPAD), F32)
    places[:, 0:MODES] = digits
    digits = places[...].astype(BF16)
    mode_row = iota((KPAD, TRIPS_PAD), 0)
    hit_in = jnp.where(mode_row == trip[0:1, :], 1.0, 0.0).astype(BF16)
    look_in = jnp.dot(digits, hit_in, preferred_element_type=F32)
    hit_out = jnp.where(mode_row == trip[1:2, :], 1.0, 0.0).astype(BF16)
    look_out = jnp.dot(digits, hit_out, preferred_element_type=F32)
    look_in = look_in.T
    column_t = look_in[:, 0:1] * 16.0 + look_in[:, 1:2]
    place_t = (look_out[2:3] * 16.0 + look_out[3:4]).astype(jnp.int32)
    key_t = jnp.where(place_t < ROWS, trip[2:3, :] * ROWS + place_t, -1)
    trip[3:4, :] = key_t
    lane_number = iota((TRIPS_PAD, KPAD), 1).astype(F32)
    by_column = jnp.where(lane_number == column_t, 1.0, 0.0).astype(BF16)

    @pl.loop(0, TERMS)
    def _(i):
        rows = iota((ROWS, TRIPS_PAD), 0) + i * ROWS
        part = jnp.where(rows == trip[3:4, :], table[0:1, :], 0.0).astype(BF16)
        onehot[pl.ds(pl.multiple_of(i * ROWS, 16), ROWS), :] = part

    vb[288:KPAD, :] = jnp.zeros((KPAD - 288, 768), BF16)
    svb[288:KPAD, :] = jnp.zeros((KPAD - 288, 512), BF16)
    svb[KPAD + 288 :, :] = jnp.zeros((KPAD - 288, 512), BF16)

    inside_up = jnp.where(zi < nz - 1, 1.0, 0.0)
    inside_down = jnp.where(zi > 0, 1.0, 0.0)

    relays = []
    for ky in (0, 1, 3, 2):
        first = 1 if ky == 0 else 0
        here = got.at[core, pl.ds(ky * SIDE + first, SIDE - first)]
        pltpu.make_async_copy(here, here, recv1.at[ky]).wait()
        line = got.at[core, pl.ds(ky * SIDE, SIDE)]
        copy = pltpu.make_async_remote_copy(
            src_ref=line, dst_ref=line, send_sem=sendr.at[ky], recv_sem=recvr.at[ky],
            device_id=(twin, zi), device_id_type=MESH,
        )
        copy.start()
        relays.append(copy)

    def unpack(half):
        most = pl.ds(pl.multiple_of(half * 128, 128), 128)
        rest = pl.ds(pl.multiple_of(256 + half * 16, 16), 16)
        for pair in range(3):
            both = got[half, :, pair * 16 : pair * 16 + 16, :].astype(F32)
            vf[pair * 2, most, :] = both[:, :8, :].reshape(128, 128)
            if pair < 2:
                vf[pair * 2 + 1, most, :] = both[:, 8:, :].reshape(128, 128)
            else:
                ninth[...] = both[:, 8:, :].reshape(128, 128)
        for j in range(5):
            vf[j, rest, :] = ninth[pl.ds(j, 16, stride=8), :]
            vb[most, j * 128 : j * 128 + 128] = vf[j, most, :].astype(BF16)
            vb[rest, j * 128 : j * 128 + 128] = vf[j, rest, :].astype(BF16)
        return most, rest

    @pl.when(odd == 0)
    def _():
        pl.semaphore_wait(ready, len(around))
        for copy in k_copies:
            copy.start()

    most, rest = unpack(core)
    edges = jnp.concatenate(
        [
            jnp.dot(vb[most, 0:512], gather_edge, preferred_element_type=F32),
            jnp.dot(vb[rest, 0:512], gather_edge, preferred_element_type=F32),
            jnp.zeros((16, 128), F32),
        ],
        axis=0,
    )
    low80 = iota((80, 128), 1) < 64
    eo[0] = jnp.where(low80, edges[:80], pltpu.roll(edges[80:], 64, 1)).astype(BF16)
    eo[1] = jnp.where(low80, pltpu.roll(edges[:80], 64, 1), edges[80:]).astype(BF16)
    z_copies = []
    for n, who, other in around:
        cross = 0 if who is me else 1
        copy = pltpu.make_async_remote_copy(
            src_ref=eo.at[n], dst_ref=ezi.at[n, core], send_sem=sendz.at[n, cross], recv_sem=recvz.at[n, cross],
            device_id=(who, other), device_id_type=MESH,
        )
        copy.start()
        z_copies.append(copy)
    p0, p1 = iota((128, 128), 0), iota((128, 128), 1)
    dz, dy = (p0 // 8) % 8 - (p1 // 8) % 8, p0 % 8 - p1 % 8
    near = (p0 // 64 == p1 // 64) & (dz * dz + dy * dy == 1)
    near = jnp.where(near, 1.0, 0.0).astype(BF16)

    def neighbours(rows, low_rows):
        for j in range(4):
            total = jnp.dot(vb[rows, j * 128 : j * 128 + 128], near, preferred_element_type=F32)
            total = total + x_sum(lambda n: vf[n, rows, :], j)
            high, remainder = split(total, 2)
            svb[rows, j * 128 : j * 128 + 128] = high
            svb[low_rows, j * 128 : j * 128 + 128] = remainder

    def shifted_rows(half):
        return (
            pl.ds(pl.multiple_of(KPAD + half * 128, 128), 128),
            pl.ds(pl.multiple_of(KPAD + 256 + half * 16, 16), 16),
        )

    low_most, low_rest = shifted_rows(core)
    neighbours(most, low_most)
    neighbours(rest, low_rest)

    coupling = jnp.dot(onehot[...], by_column, preferred_element_type=F32).astype(BF16)
    cc[:, 0:KPAD] = coupling
    cc[:, KPAD:] = coupling

    for copy in relays:
        copy.wait()
    most, rest = unpack(1 - core)
    low_most, low_rest = shifted_rows(1 - core)
    neighbours(most, low_most)
    neighbours(rest, low_rest)

    wbuf[...] = jnp.dot(cc[:, 0:KPAD], vb[:, 0:640], preferred_element_type=F32)

    ubuf[...] = jnp.dot(cc[...], svb[...], preferred_element_type=F32)

    for copy in k_copies:
        copy.wait()
    lane16 = iota((16, 128), 1)
    k_beyond = jnp.where(lane16 < 64, kzi[0] * inside_up, kzi[1] * inside_down)
    hzc[...] = pltpu.roll(edge, 64, 1) + k_beyond
    hxc[...] = jnp.where(lane16 < 64, k_tile(0), k_tile(3)) + k_tile(4)
    spread = jnp.zeros((16, 512), F32)
    for piece in reversed(split(k_beyond, 3)):
        spread = spread + jnp.dot(piece, spread_edge, preferred_element_type=F32)
    for j in range(4):
        total = 6.0 * k_tile(j) + x_sum(k_tile, j) + yz_sum(k_tile(j)) + spread[:, j * 128 : j * 128 + 128]
        if j == 0:
            total = total + jnp.where(lane16 < 64, k_tile(4), 0.0)
        if j == 3:
            total = total + jnp.where(lane16 >= 64, k_tile(4), 0.0)
        ka[j] = total

    @pl.loop(0, ROWS // 16)
    def _(block):
        acc = [jnp.zeros((16, 128), F32) for _ in range(4)]
        mass = [jnp.zeros((16, 128), F32) for _ in range(4)]
        side = jnp.zeros((16, 128), F32)
        for i in range(TERMS):
            at = pl.ds(pl.multiple_of(i * ROWS + block * 16, 16), 16)
            for j in range(4):
                k_row = kt[j * 16 + i : j * 16 + i + 1, :]
                w = wbuf[at, j * 128 : j * 128 + 128]
                acc[j] = acc[j] + ka[j, i : i + 1, :] * w - k_row * ubuf[at, j * 128 : j * 128 + 128]
                mass[j] = mass[j] + k_row * w
            side = side + hxc[i : i + 1, :] * wbuf[at, 512:640]
        here = pl.ds(pl.multiple_of(block * 16, 16), 16)
        for j in range(4):
            ra[j, here, :] = acc[j]
            bb[j, here, :] = mass[j]
        ex[here, :] = side

    lane = iota((ROWS, 128), 1)
    for j in range(4):
        total = ra[j] - x_sum(lambda n: bb[n], j) - yz_sum(bb[j])
        if j == 0:
            total = total - jnp.where(lane < 64, ex[...], 0.0)
        if j == 3:
            total = total - jnp.where(lane >= 64, ex[...], 0.0)
        main[j] = total

    for copy in z_copies:
        copy.wait()
    for half in range(2):
        above = ezi[0, half].astype(F32) * inside_up
        below = ezi[1, half].astype(F32) * inside_down
        one = jnp.where(low80, above, pltpu.roll(below, 64, 1)).astype(BF16)
        two = jnp.where(low80, pltpu.roll(above, 64, 1), below).astype(BF16)
        vb[half * 128 : half * 128 + 80, 640:768] = one
        vb[half * 128 + 80 : half * 128 + 128, 640:768] = two[:48]
        vb[256 + half * 16 : 272 + half * 16, 640:768] = two[48:64]
    hbuf[...] = jnp.dot(cc[:, 0:KPAD], vb[:, 640:768], preferred_element_type=F32)

    @pl.loop(0, ROWS // 16)
    def _(block):
        ends = jnp.zeros((16, 128), F32)
        for i in range(TERMS):
            at = pl.ds(pl.multiple_of(i * ROWS + block * 16, 16), 16)
            ends = ends + hzc[i : i + 1, :] * hbuf[at, :]
        ez[pl.ds(pl.multiple_of(block * 16, 16), 16), :] = ends

    end_parts = jnp.zeros((ROWS, 512), F32)
    for piece in reversed(split(ez[...], 2)):
        end_parts = end_parts + jnp.dot(piece, spread_edge, preferred_element_type=F32)
    for j in range(4):
        total = main[j] - end_parts[:, j * 128 : j * 128 + 128]
        total = 0.5 * total
        for c in range(CHIPS):
            ans[c * ANS + j * 8 : c * ANS + j * 8 + 8, :] = total[c * 8 : c * 8 + 8]
        ans[pl.ds(32 + j, CHIPS, stride=ANS), :] = total[128:ROWS]
    for j in range(4, 8):
        ans[pl.ds(32 + j, CHIPS, stride=ANS), :] = jnp.zeros((CHIPS, 128), F32)

    def block_of(c):
        return pl.ds(pl.multiple_of(c * ANS, 8), ANS)

    for ky, kx in offsets:
        target = chip_at(ky, kx)
        pltpu.make_async_remote_copy(
            src_ref=ans.at[block_of(target), :], dst_ref=ret.at[block_of(chip), :], send_sem=send2, recv_sem=recv2,
            device_id=(target * 2 + core, zi), device_id_type=MESH,
        ).start()
    ret[block_of(chip), :] = ans[block_of(chip), :]
    rest = ret.at[pl.ds(0, (CHIPS - 1) * ANS), :]
    pltpu.make_async_copy(rest, rest, recv2).wait()

    low16 = iota((CHIPS, 128), 1) < 64
    for first in range(0, OWN, 2):
        second = min(first + 1, OWN - 1)
        for j in range(4):
            one = ret[pl.ds(j * 8 + first if first < 8 else 32 + j, CHIPS, stride=ANS), :]
            two = ret[pl.ds(j * 8 + second if second < 8 else 32 + j, CHIPS, stride=ANS), :]
            turn[pl.ds(j, CHIPS, stride=8), :] = jnp.where(low16, one, pltpu.roll(two, 64, 1))
            turn[pl.ds(4 + j, CHIPS, stride=8), :] = jnp.where(low16, pltpu.roll(one, 64, 1), two)
        turned = turn[...].T
        o_ref[first] = turned[:64].reshape(8, 8, 128)
        if second > first:
            o_ref[second] = turned[64:].reshape(8, 8, 128)

    sent = msg.at[pl.ds(0, CHIPS - 1)]
    pltpu.make_async_copy(sent, sent, send1).wait()
    pltpu.make_async_copy(rest, rest, send2).wait()


def body(mode_field, kl_coeff, mode_slot, trip_kl, trip_in, trip_out, trip_weight):
    vmem = pl.BlockSpec(memory_space=pltpu.VMEM)
    operands = (mode_field, kl_coeff, mode_slot, trip_kl, trip_in, trip_out, trip_weight)
    dma = pltpu.SemaphoreType.DMA
    call = pl.pallas_call(
        kernel,
        out_shape=jax.ShapeDtypeStruct(mode_field.shape, F32),
        in_specs=[pl.BlockSpec(memory_space=pltpu.HBM)] * 7,
        out_specs=vmem,
        scratch_shapes=[
            *(pltpu.VMEM(a.shape, a.dtype) for a in operands),
            pltpu.VMEM((CHIPS * 64, 128), F32),
            pltpu.VMEM((CHIPS, MSG, 128), BF16),
            pltpu.VMEM((2, CHIPS, MSG, 128), BF16),
            pltpu.VMEM((128, 128), F32),
            pltpu.VMEM((5, 288, 128), F32),
            pltpu.VMEM((KPAD, 768), BF16),
            pltpu.VMEM((2 * KPAD, 512), BF16),
            pltpu.VMEM((TERMS * ROWS, TRIPS_PAD), BF16),
            pltpu.VMEM((TERMS * ROWS, 2 * KPAD), BF16),
            pltpu.VMEM((TERMS * ROWS, 640), F32),
            pltpu.VMEM((TERMS * ROWS, 512), F32),
            pltpu.VMEM((TERMS * ROWS, 128), F32),
            pltpu.VMEM((4, ROWS, 128), F32),
            pltpu.VMEM((128, 128), F32),
            pltpu.VMEM((4, 16, 128), F32),
            pltpu.VMEM((16, 128), F32),
            pltpu.VMEM((2, 16, 128), F32),
            pltpu.VMEM((16, 128), F32),
            pltpu.VMEM((16, 128), F32),
            pltpu.VMEM((2, 80, 128), BF16),
            pltpu.VMEM((2, 2, 80, 128), BF16),
            pltpu.VMEM((4, ROWS, 128), F32),
            pltpu.VMEM((4, ROWS, 128), F32),
            pltpu.VMEM((ROWS, 128), F32),
            pltpu.VMEM((ROWS, 128), F32),
            pltpu.VMEM((CHIPS * ANS, 128), F32),
            pltpu.VMEM((CHIPS * ANS, 128), F32),
            pltpu.VMEM((128, 128), F32),
            pltpu.VMEM((16, KPAD), F32),
            pltpu.VMEM((8, TRIPS_PAD), jnp.int32),
            pltpu.VMEM((8, TRIPS_PAD), F32),
            dma((7,)), pltpu.SemaphoreType.REGULAR, dma, dma((SIDE,)), dma((SIDE,)), dma((SIDE,)), dma((2,)), dma((2,)), dma((2, 2)), dma((2, 2)), dma, dma,
        ],
        compiler_params=pltpu.CompilerParams(
            collective_id=0, has_side_effects=True, vmem_limit_bytes=40 << 20
        ),
    )
    return call(*(pltpu.with_memory_space_constraint(a, pltpu.HBM) for a in operands))


def solution(mesh):
    placed = (P("mode", "space", None, None), P(None, "space", None, None), P(), P(), P(), P(), P())
    return jax.shard_map(
        body, mesh=mesh, in_specs=placed, out_specs=P("mode", "space", None, None), check_vma=False
    )
```

```python
import jax
import jax.numpy as jnp
from jax import lax
from jax.experimental import pallas as pl
from jax.experimental.pallas import tpu as pltpu
from jax.sharding import PartitionSpec as P

MESH = pl.DeviceIdType.MESH
F32 = jnp.float32
BF16 = jnp.bfloat16
NT = (((1,), (1,)), ((), ()))

SIDE = 4
CHIPS = 16
OWN = 9
TERMS = 11
TRIPS = 1606
TRIPS_PAD = 1664
MODES = 286
ROWS = 144
KPAD = 384
MSG = 48
ANS = 40


def iota(shape, dim):
    return lax.broadcasted_iota(jnp.int32, shape, dim)


def lane_of(value):
    return iota(value.shape, value.ndim - 1)


def split(value, parts):
    out = []
    for _ in range(parts):
        piece = value.astype(BF16)
        out.append(piece)
        value = value - piece.astype(F32)
    return out


def yz_sum(value):
    lane = lane_of(value)
    y = lane % 8
    z = (lane // 8) % 8
    total = jnp.where(y > 0, pltpu.roll(value, 1, 1), 0.0)
    total = total + jnp.where(y < 7, pltpu.roll(value, 127, 1), 0.0)
    total = total + jnp.where(z > 0, pltpu.roll(value, 8, 1), 0.0)
    return total + jnp.where(z < 7, pltpu.roll(value, 120, 1), 0.0)


def x_sum(tiles, j):
    lane = lane_of(tiles(0))
    left = tiles(j - 1) if j > 0 else jnp.where(lane >= 64, pltpu.roll(tiles(3), 64, 1), 0.0)
    right = tiles(j + 1) if j < 3 else jnp.where(lane < 64, pltpu.roll(tiles(0), 64, 1), 0.0)
    return left + right


def column_select(rows, chip, half, j):
    target = 8 * chip + j + 4 * half
    target = jnp.where(j == 4, jnp.where(half == 0, 8 * chip - 1, 8 * chip + 8), target)
    target = jnp.where(j > 4, -1, target)
    return jnp.where(iota((rows, 128), 1) == target, 1.0, 0.0).astype(BF16)


def edge_gather():
    row = iota((512, 128), 0)
    out = iota((512, 128), 1)
    j, half, z, y = row // 128, (row // 64) % 2, (row // 8) % 8, row % 8
    place = (j + 4 * half) * 8 + y
    hit = ((z == 0) & (out == place)) | ((z == 7) & (out == 64 + place))
    return jnp.where(hit, 1.0, 0.0).astype(BF16)


def edge_spread():
    out = iota((128, 512), 1)
    row = iota((128, 512), 0)
    j, half, z, y = out // 128, (out // 64) % 2, (out // 8) % 8, out % 8
    place = (j + 4 * half) * 8 + y
    hit = ((z == 7) & (row == place)) | ((z == 0) & (row == 64 + place))
    return jnp.where(hit, 1.0, 0.0).astype(BF16)


def kernel(
    v_hbm, k_hbm, slot_hbm, kl_hbm, in_hbm, out_hbm, w_hbm, o_ref,
    v_ref, k_ref, slot_ref, kl_ref, in_ref, out_ref, w_ref,
    pack, msg, got, ninth, vf, vb, svb, onehot, cc, wbuf, ubuf, hbuf, main,
    kt, ka, eok, kzi, hxc, hzc, eo, ezi, ra, bb, ex, ez, ans, ret, turn, places, trip, table,
    load, ready, send1, recv1, sendr, recvr, sendk, recvk, sendz, recvz, send2, recv2,
):
    loads = [
        pltpu.make_async_copy(src, dst, load.at[n])
        for n, (src, dst) in enumerate((
            (v_hbm, v_ref), (in_hbm, in_ref), (out_hbm, out_ref), (kl_hbm, kl_ref), (slot_hbm, slot_ref),
            (w_hbm, w_ref), (k_hbm, k_ref),
        ))
    ]
    loads[0].start()

    me = lax.axis_index("mode")
    zi = lax.axis_index("space")
    nz = lax.axis_size("space")
    chip, core = me // 2, me % 2
    ypos, xpos = chip // SIDE, chip % SIDE

    offsets = [(ky, kx) for ky in range(SIDE) for kx in range(SIDE) if (ky, kx) != (0, 0)]
    offsets.sort(key=lambda o: -(min(o[0], SIDE - o[0]) + min(o[1], SIDE - o[1])))

    def chip_at(ky, kx):
        return lax.rem(ypos + ky, SIDE) * SIDE + lax.rem(xpos + kx, SIDE)

    up, down = lax.rem(zi + 1, nz), lax.rem(zi + nz - 1, nz)

    barrier = pltpu.get_barrier_semaphore()
    twin = chip * 2 + 1 - core
    around = [(n, who, other) for n, other in enumerate((down, up)) for who in (me, twin)]
    for ky, kx in offsets:
        pl.semaphore_signal(barrier, inc=1, device_id=(chip_at(ky, kx) * 2 + core, zi), device_id_type=MESH)
    pl.semaphore_signal(barrier, inc=1, device_id=(twin, zi), device_id_type=MESH)

    odd = lax.rem(zi, 2)

    @pl.when(odd == 0)
    def _():
        for _, who, other in around:
            pl.semaphore_signal(barrier, inc=1, device_id=(who, other), device_id_type=MESH)

    for copy in loads[1:]:
        copy.start()

    row = iota((256, 128), 0)
    select = column_select(256, (row % 128) // 8, row // 128, row % 8)
    low = iota((128, 128), 1) < 64
    loads[0].wait()
    for m in range(OWN):
        field = v_ref[m].astype(F32).reshape(64, 128)
        field = jnp.concatenate([field, field], axis=0).astype(BF16)
        turned = lax.dot_general(select, field, NT, preferred_element_type=F32)
        turned = jnp.where(low, turned[:128], turned[128:])
        for c in range(CHIPS):
            if m < 8:
                pack[pl.ds(c * 64 + m, 8, stride=8), :] = turned[c * 8 : c * 8 + 8]
            else:
                pack[pl.ds(c * 64 + 40, 8), :] = turned[c * 8 : c * 8 + 8]
    for c in range(CHIPS):
        msg[c] = pack[pl.ds(c * 64, MSG), :].astype(BF16)
    got[core, 0] = msg[chip]

    pl.semaphore_wait(barrier, len(offsets) + 1 + len(around) * odd)

    @pl.when(odd == 1)
    def _():
        for _, who, other in around:
            pl.semaphore_signal(ready, inc=1, device_id=(who, other), device_id_type=MESH)

    for ky, kx in offsets:
        target = chip_at(ky, kx)
        pltpu.make_async_remote_copy(
            src_ref=msg.at[target], dst_ref=got.at[core, ky * SIDE + kx], send_sem=send1, recv_sem=recv1.at[ky],
            device_id=(target * 2 + core, zi), device_id_type=MESH,
        ).start()

    gather_edge = edge_gather()
    spread_edge = edge_spread()
    kt[...] = jnp.zeros_like(kt)
    row16 = iota((16, 128), 0)
    select_k = column_select(16, chip, row16 // 8, row16 % 8)
    loads[6].wait()
    for i in range(TERMS):
        block = k_ref[i].reshape(64, 128)
        block = jnp.concatenate([block, block], axis=0)
        turned = jnp.zeros((16, 128), F32)
        for piece in reversed(split(block, 3)):
            turned = turned + lax.dot_general(select_k, piece, NT, preferred_element_type=F32)
        kt[pl.ds(i, 8, stride=16), :] = jnp.where(low[:8], turned[:8], turned[8:])

    def k_tile(j):
        return kt[j * 16 : j * 16 + 16, :]

    whole = jnp.concatenate([k_tile(j) for j in range(4)], axis=1)
    edge = jnp.zeros((16, 128), F32)
    for piece in reversed(split(whole, 3)):
        edge = edge + jnp.dot(piece, gather_edge, preferred_element_type=F32)
    eok[...] = edge
    k_copies = []
    for n, other in enumerate((down, up)):
        copy = pltpu.make_async_remote_copy(
            src_ref=eok, dst_ref=kzi.at[n], send_sem=sendk.at[n], recv_sem=recvk.at[n],
            device_id=(me, other), device_id_type=MESH,
        )
        k_copies.append(copy)

    @pl.when(odd == 1)
    def _():
        for copy in k_copies:
            copy.start()


    for copy in loads[1:6]:
        copy.wait()
    trip[...] = jnp.full(trip.shape, -1, jnp.int32)
    trip[0:1, 0:TRIPS] = in_ref[...].reshape(1, TRIPS)
    trip[1:2, 0:TRIPS] = out_ref[...].reshape(1, TRIPS)
    trip[2:3, 0:TRIPS] = kl_ref[...].reshape(1, TRIPS)
    table[...] = jnp.zeros(table.shape, F32)
    table[0:1, 0:TRIPS] = w_ref[...].astype(F32).reshape(1, TRIPS)
    slots = jnp.broadcast_to(slot_ref[...].reshape(1, MODES), (16, MODES))
    dev = lax.shift_right_logical(slots * 57, 9)
    kind = slots - dev * OWN
    away_y = (ypos - dev // 8 + SIDE) % SIDE
    away_x = (xpos - (dev // 2) % SIDE + SIDE) % SIDE
    came = (dev % 2) * CHIPS + away_y * SIDE + away_x
    column = jnp.where(kind < 8, came * 8 + kind, 256 + came)
    place = jnp.where(kind < 8, (dev // 2) * 8 + kind, 128 + dev // 2)
    place = jnp.where(dev % 2 == core, place, 240)
    row16m = iota((16, MODES), 0)
    number = jnp.where(row16m < 2, column, place)
    digits = jnp.where(row16m % 2 == 0, lax.shift_right_logical(number, 4), number & 15)
    digits = jnp.where(row16m < 4, digits, 0).astype(F32)
    places[...] = jnp.zeros((16, KPAD), F32)
    places[:, 0:MODES] = digits
    digits = places[...].astype(BF16)
    mode_row = iota((KPAD, TRIPS_PAD), 0)
    hit_in = jnp.where(mode_row == trip[0:1, :], 1.0, 0.0).astype(BF16)
    look_in = jnp.dot(digits, hit_in, preferred_element_type=F32)
    hit_out = jnp.where(mode_row == trip[1:2, :], 1.0, 0.0).astype(BF16)
    look_out = jnp.dot(digits, hit_out, preferred_element_type=F32)
    look_in = look_in.T
    column_t = look_in[:, 0:1] * 16.0 + look_in[:, 1:2]
    place_t = (look_out[2:3] * 16.0 + look_out[3:4]).astype(jnp.int32)
    key_t = jnp.where(place_t < ROWS, trip[2:3, :] * ROWS + place_t, -1)
    trip[3:4, :] = key_t
    lane_number = iota((TRIPS_PAD, KPAD), 1).astype(F32)
    by_column = jnp.where(lane_number == column_t, 1.0, 0.0).astype(BF16)

    @pl.loop(0, TERMS)
    def _(i):
        rows = iota((ROWS, TRIPS_PAD), 0) + i * ROWS
        part = jnp.where(rows == trip[3:4, :], table[0:1, :], 0.0).astype(BF16)
        onehot[pl.ds(pl.multiple_of(i * ROWS, 16), ROWS), :] = part

    vb[288:KPAD, :] = jnp.zeros((KPAD - 288, 768), BF16)
    svb[288:KPAD, :] = jnp.zeros((KPAD - 288, 512), BF16)
    svb[KPAD + 288 :, :] = jnp.zeros((KPAD - 288, 512), BF16)

    inside_up = jnp.where(zi < nz - 1, 1.0, 0.0)
    inside_down = jnp.where(zi > 0, 1.0, 0.0)

    relays = []
    for ky in (0, 1, 3, 2):
        first = 1 if ky == 0 else 0
        here = got.at[core, pl.ds(ky * SIDE + first, SIDE - first)]
        pltpu.make_async_copy(here, here, recv1.at[ky]).wait()
        line = got.at[core, pl.ds(ky * SIDE, SIDE)]
        copy = pltpu.make_async_remote_copy(
            src_ref=line, dst_ref=line, send_sem=sendr.at[ky], recv_sem=recvr.at[ky],
            device_id=(twin, zi), device_id_type=MESH,
        )
        copy.start()
        relays.append(copy)

    def unpack(half):
        most = pl.ds(pl.multiple_of(half * 128, 128), 128)
        rest = pl.ds(pl.multiple_of(256 + half * 16, 16), 16)
        for pair in range(3):
            both = got[half, :, pair * 16 : pair * 16 + 16, :].astype(F32)
            vf[pair * 2, most, :] = both[:, :8, :].reshape(128, 128)
            if pair < 2:
                vf[pair * 2 + 1, most, :] = both[:, 8:, :].reshape(128, 128)
            else:
                ninth[...] = both[:, 8:, :].reshape(128, 128)
        for j in range(5):
            vf[j, rest, :] = ninth[pl.ds(j, 16, stride=8), :]
            vb[most, j * 128 : j * 128 + 128] = vf[j, most, :].astype(BF16)
            vb[rest, j * 128 : j * 128 + 128] = vf[j, rest, :].astype(BF16)
        return most, rest

    most, rest = unpack(core)
    edges = jnp.concatenate(
        [
            jnp.dot(vb[most, 0:512], gather_edge, preferred_element_type=F32),
            jnp.dot(vb[rest, 0:512], gather_edge, preferred_element_type=F32),
            jnp.zeros((16, 128), F32),
        ],
        axis=0,
    )
    low80 = iota((80, 128), 1) < 64
    eo[0] = jnp.where(low80, edges[:80], pltpu.roll(edges[80:], 64, 1)).astype(BF16)
    eo[1] = jnp.where(low80, pltpu.roll(edges[:80], 64, 1), edges[80:]).astype(BF16)
    z_copies = []
    for n, who, other in around:
        cross = 0 if who is me else 1
        copy = pltpu.make_async_remote_copy(
            src_ref=eo.at[n], dst_ref=ezi.at[n, core], send_sem=sendz.at[n, cross], recv_sem=recvz.at[n, cross],
            device_id=(who, other), device_id_type=MESH,
        )
        z_copies.append(copy)

    @pl.when(odd == 1)
    def _():
        for copy in z_copies:
            copy.start()

    p0, p1 = iota((128, 128), 0), iota((128, 128), 1)
    dz, dy = (p0 // 8) % 8 - (p1 // 8) % 8, p0 % 8 - p1 % 8
    near = (p0 // 64 == p1 // 64) & (dz * dz + dy * dy == 1)
    near = jnp.where(near, 1.0, 0.0).astype(BF16)

    def neighbours(rows, low_rows):
        for j in range(4):
            total = jnp.dot(vb[rows, j * 128 : j * 128 + 128], near, preferred_element_type=F32)
            total = total + x_sum(lambda n: vf[n, rows, :], j)
            high, remainder = split(total, 2)
            svb[rows, j * 128 : j * 128 + 128] = high
            svb[low_rows, j * 128 : j * 128 + 128] = remainder

    def shifted_rows(half):
        return (
            pl.ds(pl.multiple_of(KPAD + half * 128, 128), 128),
            pl.ds(pl.multiple_of(KPAD + 256 + half * 16, 16), 16),
        )

    low_most, low_rest = shifted_rows(core)
    neighbours(most, low_most)
    neighbours(rest, low_rest)

    coupling = jnp.dot(onehot[...], by_column, preferred_element_type=F32).astype(BF16)
    cc[:, 0:KPAD] = coupling
    cc[:, KPAD:] = coupling

    for copy in relays:
        copy.wait()
    most, rest = unpack(1 - core)
    low_most, low_rest = shifted_rows(1 - core)
    neighbours(most, low_most)
    neighbours(rest, low_rest)

    @pl.when(odd == 0)
    def _():
        pl.semaphore_wait(ready, len(around))
        for copy in k_copies + z_copies:
            copy.start()

    wbuf[...] = jnp.dot(cc[:, 0:KPAD], vb[:, 0:640], preferred_element_type=F32)

    ubuf[...] = jnp.dot(cc[...], svb[...], preferred_element_type=F32)

    for copy in k_copies:
        copy.wait()
    lane16 = iota((16, 128), 1)
    k_beyond = jnp.where(lane16 < 64, kzi[0] * inside_up, kzi[1] * inside_down)
    hzc[...] = pltpu.roll(edge, 64, 1) + k_beyond
    hxc[...] = jnp.where(lane16 < 64, k_tile(0), k_tile(3)) + k_tile(4)
    spread = jnp.zeros((16, 512), F32)
    for piece in reversed(split(k_beyond, 3)):
        spread = spread + jnp.dot(piece, spread_edge, preferred_element_type=F32)
    for j in range(4):
        total = 6.0 * k_tile(j) + x_sum(k_tile, j) + yz_sum(k_tile(j)) + spread[:, j * 128 : j * 128 + 128]
        if j == 0:
            total = total + jnp.where(lane16 < 64, k_tile(4), 0.0)
        if j == 3:
            total = total + jnp.where(lane16 >= 64, k_tile(4), 0.0)
        ka[j] = total

    @pl.loop(0, ROWS // 16)
    def _(block):
        acc = [jnp.zeros((16, 128), F32) for _ in range(4)]
        mass = [jnp.zeros((16, 128), F32) for _ in range(4)]
        side = jnp.zeros((16, 128), F32)
        for i in range(TERMS):
            at = pl.ds(pl.multiple_of(i * ROWS + block * 16, 16), 16)
            for j in range(4):
                k_row = kt[j * 16 + i : j * 16 + i + 1, :]
                w = wbuf[at, j * 128 : j * 128 + 128]
                acc[j] = acc[j] + ka[j, i : i + 1, :] * w - k_row * ubuf[at, j * 128 : j * 128 + 128]
                mass[j] = mass[j] + k_row * w
            side = side + hxc[i : i + 1, :] * wbuf[at, 512:640]
        here = pl.ds(pl.multiple_of(block * 16, 16), 16)
        for j in range(4):
            ra[j, here, :] = acc[j]
            bb[j, here, :] = mass[j]
        ex[here, :] = side

    lane = iota((ROWS, 128), 1)
    for j in range(4):
        total = ra[j] - x_sum(lambda n: bb[n], j) - yz_sum(bb[j])
        if j == 0:
            total = total - jnp.where(lane < 64, ex[...], 0.0)
        if j == 3:
            total = total - jnp.where(lane >= 64, ex[...], 0.0)
        main[j] = total

    for copy in z_copies:
        copy.wait()
    for half in range(2):
        above = ezi[0, half].astype(F32) * inside_up
        below = ezi[1, half].astype(F32) * inside_down
        one = jnp.where(low80, above, pltpu.roll(below, 64, 1)).astype(BF16)
        two = jnp.where(low80, pltpu.roll(above, 64, 1), below).astype(BF16)
        vb[half * 128 : half * 128 + 80, 640:768] = one
        vb[half * 128 + 80 : half * 128 + 128, 640:768] = two[:48]
        vb[256 + half * 16 : 272 + half * 16, 640:768] = two[48:64]
    hbuf[...] = jnp.dot(cc[:, 0:KPAD], vb[:, 640:768], preferred_element_type=F32)

    @pl.loop(0, ROWS // 16)
    def _(block):
        ends = jnp.zeros((16, 128), F32)
        for i in range(TERMS):
            at = pl.ds(pl.multiple_of(i * ROWS + block * 16, 16), 16)
            ends = ends + hzc[i : i + 1, :] * hbuf[at, :]
        ez[pl.ds(pl.multiple_of(block * 16, 16), 16), :] = ends

    end_parts = jnp.zeros((ROWS, 512), F32)
    for piece in reversed(split(ez[...], 2)):
        end_parts = end_parts + jnp.dot(piece, spread_edge, preferred_element_type=F32)
    for j in range(4):
        total = main[j] - end_parts[:, j * 128 : j * 128 + 128]
        total = 0.5 * total
        for c in range(CHIPS):
            ans[c * ANS + j * 8 : c * ANS + j * 8 + 8, :] = total[c * 8 : c * 8 + 8]
        ans[pl.ds(32 + j, CHIPS, stride=ANS), :] = total[128:ROWS]
    for j in range(4, 8):
        ans[pl.ds(32 + j, CHIPS, stride=ANS), :] = jnp.zeros((CHIPS, 128), F32)

    def block_of(c):
        return pl.ds(pl.multiple_of(c * ANS, 8), ANS)

    for ky, kx in offsets:
        target = chip_at(ky, kx)
        pltpu.make_async_remote_copy(
            src_ref=ans.at[block_of(target), :], dst_ref=ret.at[block_of(chip), :], send_sem=send2, recv_sem=recv2,
            device_id=(target * 2 + core, zi), device_id_type=MESH,
        ).start()
    ret[block_of(chip), :] = ans[block_of(chip), :]
    rest = ret.at[pl.ds(0, (CHIPS - 1) * ANS), :]
    pltpu.make_async_copy(rest, rest, recv2).wait()

    low16 = iota((CHIPS, 128), 1) < 64
    for first in range(0, OWN, 2):
        second = min(first + 1, OWN - 1)
        for j in range(4):
            one = ret[pl.ds(j * 8 + first if first < 8 else 32 + j, CHIPS, stride=ANS), :]
            two = ret[pl.ds(j * 8 + second if second < 8 else 32 + j, CHIPS, stride=ANS), :]
            turn[pl.ds(j, CHIPS, stride=8), :] = jnp.where(low16, one, pltpu.roll(two, 64, 1))
            turn[pl.ds(4 + j, CHIPS, stride=8), :] = jnp.where(low16, pltpu.roll(one, 64, 1), two)
        turned = turn[...].T
        o_ref[first] = turned[:64].reshape(8, 8, 128)
        if second > first:
            o_ref[second] = turned[64:].reshape(8, 8, 128)

    sent = msg.at[pl.ds(0, CHIPS - 1)]
    pltpu.make_async_copy(sent, sent, send1).wait()
    pltpu.make_async_copy(rest, rest, send2).wait()


def body(mode_field, kl_coeff, mode_slot, trip_kl, trip_in, trip_out, trip_weight):
    vmem = pl.BlockSpec(memory_space=pltpu.VMEM)
    operands = (mode_field, kl_coeff, mode_slot, trip_kl, trip_in, trip_out, trip_weight)
    dma = pltpu.SemaphoreType.DMA
    call = pl.pallas_call(
        kernel,
        out_shape=jax.ShapeDtypeStruct(mode_field.shape, F32),
        in_specs=[pl.BlockSpec(memory_space=pltpu.HBM)] * 7,
        out_specs=vmem,
        scratch_shapes=[
            *(pltpu.VMEM(a.shape, a.dtype) for a in operands),
            pltpu.VMEM((CHIPS * 64, 128), F32),
            pltpu.VMEM((CHIPS, MSG, 128), BF16),
            pltpu.VMEM((2, CHIPS, MSG, 128), BF16),
            pltpu.VMEM((128, 128), F32),
            pltpu.VMEM((5, 288, 128), F32),
            pltpu.VMEM((KPAD, 768), BF16),
            pltpu.VMEM((2 * KPAD, 512), BF16),
            pltpu.VMEM((TERMS * ROWS, TRIPS_PAD), BF16),
            pltpu.VMEM((TERMS * ROWS, 2 * KPAD), BF16),
            pltpu.VMEM((TERMS * ROWS, 640), F32),
            pltpu.VMEM((TERMS * ROWS, 512), F32),
            pltpu.VMEM((TERMS * ROWS, 128), F32),
            pltpu.VMEM((4, ROWS, 128), F32),
            pltpu.VMEM((128, 128), F32),
            pltpu.VMEM((4, 16, 128), F32),
            pltpu.VMEM((16, 128), F32),
            pltpu.VMEM((2, 16, 128), F32),
            pltpu.VMEM((16, 128), F32),
            pltpu.VMEM((16, 128), F32),
            pltpu.VMEM((2, 80, 128), BF16),
            pltpu.VMEM((2, 2, 80, 128), BF16),
            pltpu.VMEM((4, ROWS, 128), F32),
            pltpu.VMEM((4, ROWS, 128), F32),
            pltpu.VMEM((ROWS, 128), F32),
            pltpu.VMEM((ROWS, 128), F32),
            pltpu.VMEM((CHIPS * ANS, 128), F32),
            pltpu.VMEM((CHIPS * ANS, 128), F32),
            pltpu.VMEM((128, 128), F32),
            pltpu.VMEM((16, KPAD), F32),
            pltpu.VMEM((8, TRIPS_PAD), jnp.int32),
            pltpu.VMEM((8, TRIPS_PAD), F32),
            dma((7,)), pltpu.SemaphoreType.REGULAR, dma, dma((SIDE,)), dma((SIDE,)), dma((SIDE,)), dma((2,)), dma((2,)), dma((2, 2)), dma((2, 2)), dma, dma,
        ],
        compiler_params=pltpu.CompilerParams(
            collective_id=0, has_side_effects=True, vmem_limit_bytes=40 << 20
        ),
    )
    return call(*(pltpu.with_memory_space_constraint(a, pltpu.HBM) for a in operands))


def solution(mesh):
    placed = (P("mode", "space", None, None), P(None, "space", None, None), P(), P(), P(), P(), P())
    return jax.shard_map(
        body, mesh=mesh, in_specs=placed, out_specs=P("mode", "space", None, None), check_vma=False
    )
```

```python
import jax
import jax.numpy as jnp
from jax import lax
from jax.experimental import pallas as pl
from jax.experimental.pallas import tpu as pltpu
from jax.sharding import PartitionSpec as P

MESH = pl.DeviceIdType.MESH
F32 = jnp.float32
BF16 = jnp.bfloat16
NT = (((1,), (1,)), ((), ()))

SIDE = 4
CHIPS = 16
OWN = 9
TERMS = 11
TRIPS = 1606
TRIPS_PAD = 1664
MODES = 286
ROWS = 144
KPAD = 384
MSG = 48
ANS = 40


def iota(shape, dim):
    return lax.broadcasted_iota(jnp.int32, shape, dim)


def lane_of(value):
    return iota(value.shape, value.ndim - 1)


def split(value, parts):
    out = []
    for _ in range(parts):
        piece = value.astype(BF16)
        out.append(piece)
        value = value - piece.astype(F32)
    return out


def yz_sum(value):
    lane = lane_of(value)
    y = lane % 8
    z = (lane // 8) % 8
    total = jnp.where(y > 0, pltpu.roll(value, 1, 1), 0.0)
    total = total + jnp.where(y < 7, pltpu.roll(value, 127, 1), 0.0)
    total = total + jnp.where(z > 0, pltpu.roll(value, 8, 1), 0.0)
    return total + jnp.where(z < 7, pltpu.roll(value, 120, 1), 0.0)


def x_sum(tiles, j):
    lane = lane_of(tiles(0))
    left = tiles(j - 1) if j > 0 else jnp.where(lane >= 64, pltpu.roll(tiles(3), 64, 1), 0.0)
    right = tiles(j + 1) if j < 3 else jnp.where(lane < 64, pltpu.roll(tiles(0), 64, 1), 0.0)
    return left + right


def column_select(rows, chip, half, j):
    target = 8 * chip + j + 4 * half
    target = jnp.where(j == 4, jnp.where(half == 0, 8 * chip - 1, 8 * chip + 8), target)
    target = jnp.where(j > 4, -1, target)
    return jnp.where(iota((rows, 128), 1) == target, 1.0, 0.0).astype(BF16)


def edge_gather():
    row = iota((512, 128), 0)
    out = iota((512, 128), 1)
    j, half, z, y = row // 128, (row // 64) % 2, (row // 8) % 8, row % 8
    place = (j + 4 * half) * 8 + y
    hit = ((z == 0) & (out == place)) | ((z == 7) & (out == 64 + place))
    return jnp.where(hit, 1.0, 0.0).astype(BF16)


def edge_spread():
    out = iota((128, 512), 1)
    row = iota((128, 512), 0)
    j, half, z, y = out // 128, (out // 64) % 2, (out // 8) % 8, out % 8
    place = (j + 4 * half) * 8 + y
    hit = ((z == 7) & (row == place)) | ((z == 0) & (row == 64 + place))
    return jnp.where(hit, 1.0, 0.0).astype(BF16)


def kernel(
    v_hbm, k_hbm, slot_hbm, kl_hbm, in_hbm, out_hbm, w_hbm, o_ref,
    v_ref, k_ref, slot_ref, kl_ref, in_ref, out_ref, w_ref,
    pack, msg, got, ninth, vf, vb, svb, onehot, cc, wbuf, ubuf, hbuf, main,
    kt, ka, eok, kzi, hxc, hzc, eo, ezi, ra, bb, ex, ez, ans, ret, turn, places, trip, table,
    load, ready, send1, recv1, sendr, recvr, sendk, recvk, sendz, recvz, send2, recv2,
):
    loads = [
        pltpu.make_async_copy(src, dst, load.at[n])
        for n, (src, dst) in enumerate((
            (v_hbm, v_ref), (in_hbm, in_ref), (out_hbm, out_ref), (kl_hbm, kl_ref), (slot_hbm, slot_ref),
            (w_hbm, w_ref), (k_hbm, k_ref),
        ))
    ]
    loads[0].start()

    me = lax.axis_index("mode")
    zi = lax.axis_index("space")
    nz = lax.axis_size("space")
    chip, core = me // 2, me % 2
    ypos, xpos = chip // SIDE, chip % SIDE

    offsets = [(ky, kx) for ky in range(SIDE) for kx in range(SIDE) if (ky, kx) != (0, 0)]
    offsets.sort(key=lambda o: -(min(o[0], SIDE - o[0]) + min(o[1], SIDE - o[1])))

    def chip_at(ky, kx):
        return lax.rem(ypos + ky, SIDE) * SIDE + lax.rem(xpos + kx, SIDE)

    up, down = lax.rem(zi + 1, nz), lax.rem(zi + nz - 1, nz)

    barrier = pltpu.get_barrier_semaphore()
    twin = chip * 2 + 1 - core
    around = [(n, who, other) for n, other in enumerate((down, up)) for who in (me, twin)]
    for ky, kx in offsets:
        pl.semaphore_signal(barrier, inc=1, device_id=(chip_at(ky, kx) * 2 + core, zi), device_id_type=MESH)
    pl.semaphore_signal(barrier, inc=1, device_id=(twin, zi), device_id_type=MESH)

    odd = lax.rem(zi, 2)

    @pl.when(odd == 0)
    def _():
        for _, who, other in around:
            pl.semaphore_signal(barrier, inc=1, device_id=(who, other), device_id_type=MESH)

    for copy in loads[1:]:
        copy.start()

    for j in range(4, 8):
        ans[pl.ds(32 + j, CHIPS, stride=ANS), :] = jnp.zeros((CHIPS, 128), F32)

    row = iota((256, 128), 0)
    select = column_select(256, (row % 128) // 8, row // 128, row % 8)
    low = iota((128, 128), 1) < 64
    loads[0].wait()
    for m in range(OWN):
        field = v_ref[m].astype(F32).reshape(64, 128)
        field = jnp.concatenate([field, field], axis=0).astype(BF16)
        turned = lax.dot_general(select, field, NT, preferred_element_type=F32)
        turned = jnp.where(low, turned[:128], turned[128:])
        for c in range(CHIPS):
            if m < 8:
                pack[pl.ds(c * 64 + m, 8, stride=8), :] = turned[c * 8 : c * 8 + 8]
            else:
                pack[pl.ds(c * 64 + 40, 8), :] = turned[c * 8 : c * 8 + 8]
    for c in range(CHIPS):
        msg[c] = pack[pl.ds(c * 64, MSG), :].astype(BF16)
    got[core, 0] = msg[chip]

    pl.semaphore_wait(barrier, len(offsets) + 1 + len(around) * odd)

    @pl.when(odd == 1)
    def _():
        for _, who, other in around:
            pl.semaphore_signal(ready, inc=1, device_id=(who, other), device_id_type=MESH)

    for ky, kx in offsets:
        target = chip_at(ky, kx)
        pltpu.make_async_remote_copy(
            src_ref=msg.at[target], dst_ref=got.at[core, ky * SIDE + kx], send_sem=send1, recv_sem=recv1.at[ky],
            device_id=(target * 2 + core, zi), device_id_type=MESH,
        ).start()

    gather_edge = edge_gather()
    spread_edge = edge_spread()
    kt[...] = jnp.zeros_like(kt)
    row16 = iota((16, 128), 0)
    select_k = column_select(16, chip, row16 // 8, row16 % 8)
    loads[6].wait()
    for i in range(TERMS):
        block = k_ref[i].reshape(64, 128)
        block = jnp.concatenate([block, block], axis=0)
        turned = jnp.zeros((16, 128), F32)
        for piece in reversed(split(block, 3)):
            turned = turned + lax.dot_general(select_k, piece, NT, preferred_element_type=F32)
        kt[pl.ds(i, 8, stride=16), :] = jnp.where(low[:8], turned[:8], turned[8:])

    def k_tile(j):
        return kt[j * 16 : j * 16 + 16, :]

    whole = jnp.concatenate([k_tile(j) for j in range(4)], axis=1)
    edge = jnp.zeros((16, 128), F32)
    for piece in reversed(split(whole, 3)):
        edge = edge + jnp.dot(piece, gather_edge, preferred_element_type=F32)
    eok[...] = edge
    k_copies = []
    for n, other in enumerate((down, up)):
        copy = pltpu.make_async_remote_copy(
            src_ref=eok, dst_ref=kzi.at[n], send_sem=sendk.at[n], recv_sem=recvk.at[n],
            device_id=(me, other), device_id_type=MESH,
        )
        k_copies.append(copy)

    @pl.when(odd == 1)
    def _():
        for copy in k_copies:
            copy.start()


    for copy in loads[1:6]:
        copy.wait()
    trip[...] = jnp.full(trip.shape, -1, jnp.int32)
    trip[0:1, 0:TRIPS] = in_ref[...].reshape(1, TRIPS)
    trip[1:2, 0:TRIPS] = out_ref[...].reshape(1, TRIPS)
    trip[2:3, 0:TRIPS] = kl_ref[...].reshape(1, TRIPS)
    table[...] = jnp.zeros(table.shape, F32)
    table[0:1, 0:TRIPS] = w_ref[...].astype(F32).reshape(1, TRIPS)
    slots = jnp.broadcast_to(slot_ref[...].reshape(1, MODES), (16, MODES))
    dev = lax.shift_right_logical(slots * 57, 9)
    kind = slots - dev * OWN
    away_y = (ypos - dev // 8 + SIDE) % SIDE
    away_x = (xpos - (dev // 2) % SIDE + SIDE) % SIDE
    came = (dev % 2) * CHIPS + away_y * SIDE + away_x
    column = jnp.where(kind < 8, came * 8 + kind, 256 + came)
    place = jnp.where(kind < 8, (dev // 2) * 8 + kind, 128 + dev // 2)
    place = jnp.where(dev % 2 == core, place, 240)
    row16m = iota((16, MODES), 0)
    number = jnp.where(row16m < 2, column, place)
    digits = jnp.where(row16m % 2 == 0, lax.shift_right_logical(number, 4), number & 15)
    digits = jnp.where(row16m < 4, digits, 0).astype(F32)
    places[...] = jnp.zeros((16, KPAD), F32)
    places[:, 0:MODES] = digits
    digits = places[...].astype(BF16)
    mode_row = iota((KPAD, TRIPS_PAD), 0)
    hit_in = jnp.where(mode_row == trip[0:1, :], 1.0, 0.0).astype(BF16)
    look_in = jnp.dot(digits, hit_in, preferred_element_type=F32)
    hit_out = jnp.where(mode_row == trip[1:2, :], 1.0, 0.0).astype(BF16)
    look_out = jnp.dot(digits, hit_out, preferred_element_type=F32)
    look_in = look_in.T
    column_t = look_in[:, 0:1] * 16.0 + look_in[:, 1:2]
    place_t = (look_out[2:3] * 16.0 + look_out[3:4]).astype(jnp.int32)
    key_t = jnp.where(place_t < ROWS, trip[2:3, :] * ROWS + place_t, -1)
    trip[3:4, :] = key_t
    lane_number = iota((TRIPS_PAD, KPAD), 1).astype(F32)
    by_column = jnp.where(lane_number == column_t, 1.0, 0.0).astype(BF16)

    @pl.loop(0, TERMS)
    def _(i):
        rows = iota((ROWS, TRIPS_PAD), 0) + i * ROWS
        part = jnp.where(rows == trip[3:4, :], table[0:1, :], 0.0).astype(BF16)
        onehot[pl.ds(pl.multiple_of(i * ROWS, 16), ROWS), :] = part

    vb[288:KPAD, :] = jnp.zeros((KPAD - 288, 768), BF16)
    svb[288:KPAD, :] = jnp.zeros((KPAD - 288, 512), BF16)
    svb[KPAD + 288 :, :] = jnp.zeros((KPAD - 288, 512), BF16)

    inside_up = jnp.where(zi < nz - 1, 1.0, 0.0)
    inside_down = jnp.where(zi > 0, 1.0, 0.0)

    relays = []
    for ky in (0, 1, 3, 2):
        first = 1 if ky == 0 else 0
        here = got.at[core, pl.ds(ky * SIDE + first, SIDE - first)]
        pltpu.make_async_copy(here, here, recv1.at[ky]).wait()
        line = got.at[core, pl.ds(ky * SIDE, SIDE)]
        copy = pltpu.make_async_remote_copy(
            src_ref=line, dst_ref=line, send_sem=sendr.at[ky], recv_sem=recvr.at[ky],
            device_id=(twin, zi), device_id_type=MESH,
        )
        copy.start()
        relays.append(copy)

    def unpack(half):
        most = pl.ds(pl.multiple_of(half * 128, 128), 128)
        rest = pl.ds(pl.multiple_of(256 + half * 16, 16), 16)
        for pair in range(3):
            both = got[half, :, pair * 16 : pair * 16 + 16, :].astype(F32)
            vf[pair * 2, most, :] = both[:, :8, :].reshape(128, 128)
            if pair < 2:
                vf[pair * 2 + 1, most, :] = both[:, 8:, :].reshape(128, 128)
            else:
                ninth[...] = both[:, 8:, :].reshape(128, 128)
        for j in range(5):
            vf[j, rest, :] = ninth[pl.ds(j, 16, stride=8), :]
            vb[most, j * 128 : j * 128 + 128] = vf[j, most, :].astype(BF16)
            vb[rest, j * 128 : j * 128 + 128] = vf[j, rest, :].astype(BF16)
        return most, rest

    most, rest = unpack(core)
    edges = jnp.concatenate(
        [
            jnp.dot(vb[most, 0:512], gather_edge, preferred_element_type=F32),
            jnp.dot(vb[rest, 0:512], gather_edge, preferred_element_type=F32),
            jnp.zeros((16, 128), F32),
        ],
        axis=0,
    )
    low80 = iota((80, 128), 1) < 64
    eo[0] = jnp.where(low80, edges[:80], pltpu.roll(edges[80:], 64, 1)).astype(BF16)
    eo[1] = jnp.where(low80, pltpu.roll(edges[:80], 64, 1), edges[80:]).astype(BF16)
    z_copies = []
    for n, who, other in around:
        cross = 0 if who is me else 1
        copy = pltpu.make_async_remote_copy(
            src_ref=eo.at[n], dst_ref=ezi.at[n, core], send_sem=sendz.at[n, cross], recv_sem=recvz.at[n, cross],
            device_id=(who, other), device_id_type=MESH,
        )
        z_copies.append(copy)

    @pl.when(odd == 1)
    def _():
        for copy in z_copies:
            copy.start()

    p0, p1 = iota((128, 128), 0), iota((128, 128), 1)
    dz, dy = (p0 // 8) % 8 - (p1 // 8) % 8, p0 % 8 - p1 % 8
    near = (p0 // 64 == p1 // 64) & (dz * dz + dy * dy == 1)
    near = jnp.where(near, 1.0, 0.0).astype(BF16)

    def neighbours(rows, low_rows):
        for j in range(4):
            total = jnp.dot(vb[rows, j * 128 : j * 128 + 128], near, preferred_element_type=F32)
            total = total + x_sum(lambda n: vf[n, rows, :], j)
            high, remainder = split(total, 2)
            svb[rows, j * 128 : j * 128 + 128] = high
            svb[low_rows, j * 128 : j * 128 + 128] = remainder

    def shifted_rows(half):
        return (
            pl.ds(pl.multiple_of(KPAD + half * 128, 128), 128),
            pl.ds(pl.multiple_of(KPAD + 256 + half * 16, 16), 16),
        )

    low_most, low_rest = shifted_rows(core)
    neighbours(most, low_most)
    neighbours(rest, low_rest)

    coupling = jnp.dot(onehot[...], by_column, preferred_element_type=F32).astype(BF16)
    cc[:, 0:KPAD] = coupling
    cc[:, KPAD:] = coupling

    for copy in relays:
        copy.wait()
    most, rest = unpack(1 - core)
    low_most, low_rest = shifted_rows(1 - core)
    neighbours(most, low_most)
    neighbours(rest, low_rest)

    @pl.when(odd == 0)
    def _():
        pl.semaphore_wait(ready, len(around))
        for copy in k_copies + z_copies:
            copy.start()

    wbuf[...] = jnp.dot(cc[:, 0:KPAD], vb[:, 0:640], preferred_element_type=F32)

    ubuf[...] = jnp.dot(cc[...], svb[...], preferred_element_type=F32)

    for copy in k_copies:
        copy.wait()
    lane16 = iota((16, 128), 1)
    k_beyond = jnp.where(lane16 < 64, kzi[0] * inside_up, kzi[1] * inside_down)
    hzc[...] = pltpu.roll(edge, 64, 1) + k_beyond
    hxc[...] = jnp.where(lane16 < 64, k_tile(0), k_tile(3)) + k_tile(4)
    spread = jnp.zeros((16, 512), F32)
    for piece in reversed(split(k_beyond, 3)):
        spread = spread + jnp.dot(piece, spread_edge, preferred_element_type=F32)
    for j in range(4):
        total = 6.0 * k_tile(j) + x_sum(k_tile, j) + yz_sum(k_tile(j)) + spread[:, j * 128 : j * 128 + 128]
        if j == 0:
            total = total + jnp.where(lane16 < 64, k_tile(4), 0.0)
        if j == 3:
            total = total + jnp.where(lane16 >= 64, k_tile(4), 0.0)
        ka[j] = total

    @pl.loop(0, ROWS // 16)
    def _(block):
        acc = [jnp.zeros((16, 128), F32) for _ in range(4)]
        mass = [jnp.zeros((16, 128), F32) for _ in range(4)]
        side = jnp.zeros((16, 128), F32)
        for i in range(TERMS):
            at = pl.ds(pl.multiple_of(i * ROWS + block * 16, 16), 16)
            for j in range(4):
                k_row = kt[j * 16 + i : j * 16 + i + 1, :]
                w = wbuf[at, j * 128 : j * 128 + 128]
                acc[j] = acc[j] + ka[j, i : i + 1, :] * w - k_row * ubuf[at, j * 128 : j * 128 + 128]
                mass[j] = mass[j] + k_row * w
            side = side + hxc[i : i + 1, :] * wbuf[at, 512:640]
        here = pl.ds(pl.multiple_of(block * 16, 16), 16)
        for j in range(4):
            ra[j, here, :] = acc[j]
            bb[j, here, :] = mass[j]
        ex[here, :] = side

    lane = iota((ROWS, 128), 1)
    for j in range(4):
        total = ra[j] - x_sum(lambda n: bb[n], j) - yz_sum(bb[j])
        if j == 0:
            total = total - jnp.where(lane < 64, ex[...], 0.0)
        if j == 3:
            total = total - jnp.where(lane >= 64, ex[...], 0.0)
        main[j] = total

    for copy in z_copies:
        copy.wait()
    for half in range(2):
        above = ezi[0, half].astype(F32) * inside_up
        below = ezi[1, half].astype(F32) * inside_down
        one = jnp.where(low80, above, pltpu.roll(below, 64, 1)).astype(BF16)
        two = jnp.where(low80, pltpu.roll(above, 64, 1), below).astype(BF16)
        vb[half * 128 : half * 128 + 80, 640:768] = one
        vb[half * 128 + 80 : half * 128 + 128, 640:768] = two[:48]
        vb[256 + half * 16 : 272 + half * 16, 640:768] = two[48:64]
    hbuf[...] = jnp.dot(cc[:, 0:KPAD], vb[:, 640:768], preferred_element_type=F32)

    @pl.loop(0, ROWS // 16)
    def _(block):
        ends = jnp.zeros((16, 128), F32)
        for i in range(TERMS):
            at = pl.ds(pl.multiple_of(i * ROWS + block * 16, 16), 16)
            ends = ends + hzc[i : i + 1, :] * hbuf[at, :]
        ez[pl.ds(pl.multiple_of(block * 16, 16), 16), :] = ends

    end_parts = jnp.zeros((ROWS, 512), F32)
    for piece in reversed(split(ez[...], 2)):
        end_parts = end_parts + jnp.dot(piece, spread_edge, preferred_element_type=F32)
    for j in range(4):
        total = main[j] - end_parts[:, j * 128 : j * 128 + 128]
        total = 0.5 * total
        for c in range(CHIPS):
            ans[c * ANS + j * 8 : c * ANS + j * 8 + 8, :] = total[c * 8 : c * 8 + 8]
        ans[pl.ds(32 + j, CHIPS, stride=ANS), :] = total[128:ROWS]

    def block_of(c):
        return pl.ds(pl.multiple_of(c * ANS, 8), ANS)

    for ky, kx in offsets:
        target = chip_at(ky, kx)
        pltpu.make_async_remote_copy(
            src_ref=ans.at[block_of(target), :], dst_ref=ret.at[block_of(chip), :], send_sem=send2, recv_sem=recv2,
            device_id=(target * 2 + core, zi), device_id_type=MESH,
        ).start()
    ret[block_of(chip), :] = ans[block_of(chip), :]
    rest = ret.at[pl.ds(0, (CHIPS - 1) * ANS), :]
    pltpu.make_async_copy(rest, rest, recv2).wait()

    low16 = iota((CHIPS, 128), 1) < 64
    for first in range(0, OWN, 2):
        second = min(first + 1, OWN - 1)
        base = first * 64
        for j in range(4):
            one = ret[pl.ds(j * 8 + first if first < 8 else 32 + j, CHIPS, stride=ANS), :]
            two = ret[pl.ds(j * 8 + second if second < 8 else 32 + j, CHIPS, stride=ANS), :]
            turn[pl.ds(base + j, CHIPS, stride=8), :] = jnp.where(low16, one, pltpu.roll(two, 64, 1))
            turn[pl.ds(base + 4 + j, CHIPS, stride=8), :] = jnp.where(low16, pltpu.roll(one, 64, 1), two)
    for first in range(0, OWN, 2):
        turned = turn[first * 64 : first * 64 + 128, :].T
        o_ref[first] = turned[:64].reshape(8, 8, 128)
        if first + 1 < OWN:
            o_ref[first + 1] = turned[64:].reshape(8, 8, 128)

    sent = msg.at[pl.ds(0, CHIPS - 1)]
    pltpu.make_async_copy(sent, sent, send1).wait()
    pltpu.make_async_copy(rest, rest, send2).wait()


def body(mode_field, kl_coeff, mode_slot, trip_kl, trip_in, trip_out, trip_weight):
    vmem = pl.BlockSpec(memory_space=pltpu.VMEM)
    operands = (mode_field, kl_coeff, mode_slot, trip_kl, trip_in, trip_out, trip_weight)
    dma = pltpu.SemaphoreType.DMA
    call = pl.pallas_call(
        kernel,
        out_shape=jax.ShapeDtypeStruct(mode_field.shape, F32),
        in_specs=[pl.BlockSpec(memory_space=pltpu.HBM)] * 7,
        out_specs=vmem,
        scratch_shapes=[
            *(pltpu.VMEM(a.shape, a.dtype) for a in operands),
            pltpu.VMEM((CHIPS * 64, 128), F32),
            pltpu.VMEM((CHIPS, MSG, 128), BF16),
            pltpu.VMEM((2, CHIPS, MSG, 128), BF16),
            pltpu.VMEM((128, 128), F32),
            pltpu.VMEM((5, 288, 128), F32),
            pltpu.VMEM((KPAD, 768), BF16),
            pltpu.VMEM((2 * KPAD, 512), BF16),
            pltpu.VMEM((TERMS * ROWS, TRIPS_PAD), BF16),
            pltpu.VMEM((TERMS * ROWS, 2 * KPAD), BF16),
            pltpu.VMEM((TERMS * ROWS, 640), F32),
            pltpu.VMEM((TERMS * ROWS, 512), F32),
            pltpu.VMEM((TERMS * ROWS, 128), F32),
            pltpu.VMEM((4, ROWS, 128), F32),
            pltpu.VMEM((128, 128), F32),
            pltpu.VMEM((4, 16, 128), F32),
            pltpu.VMEM((16, 128), F32),
            pltpu.VMEM((2, 16, 128), F32),
            pltpu.VMEM((16, 128), F32),
            pltpu.VMEM((16, 128), F32),
            pltpu.VMEM((2, 80, 128), BF16),
            pltpu.VMEM((2, 2, 80, 128), BF16),
            pltpu.VMEM((4, ROWS, 128), F32),
            pltpu.VMEM((4, ROWS, 128), F32),
            pltpu.VMEM((ROWS, 128), F32),
            pltpu.VMEM((ROWS, 128), F32),
            pltpu.VMEM((CHIPS * ANS, 128), F32),
            pltpu.VMEM((CHIPS * ANS, 128), F32),
            pltpu.VMEM((640, 128), F32),
            pltpu.VMEM((16, KPAD), F32),
            pltpu.VMEM((8, TRIPS_PAD), jnp.int32),
            pltpu.VMEM((8, TRIPS_PAD), F32),
            dma((7,)), pltpu.SemaphoreType.REGULAR, dma, dma((SIDE,)), dma((SIDE,)), dma((SIDE,)), dma((2,)), dma((2,)), dma((2, 2)), dma((2, 2)), dma, dma,
        ],
        compiler_params=pltpu.CompilerParams(
            collective_id=0, has_side_effects=True, vmem_limit_bytes=40 << 20
        ),
    )
    return call(*(pltpu.with_memory_space_constraint(a, pltpu.HBM) for a in operands))


def solution(mesh):
    placed = (P("mode", "space", None, None), P(None, "space", None, None), P(), P(), P(), P(), P())
    return jax.shard_map(
        body, mesh=mesh, in_specs=placed, out_specs=P("mode", "space", None, None), check_vma=False
    )
```

```python
import jax
import jax.numpy as jnp
from jax import lax
from jax.experimental import pallas as pl
from jax.experimental.pallas import tpu as pltpu
from jax.sharding import PartitionSpec as P

MESH = pl.DeviceIdType.MESH
F32 = jnp.float32
BF16 = jnp.bfloat16
NT = (((1,), (1,)), ((), ()))

SIDE = 4
CHIPS = 16
OWN = 9
TERMS = 11
TRIPS = 1606
TRIPS_PAD = 1664
MODES = 286
ROWS = 144
KPAD = 384
MSG = 48
ANS = 40


def iota(shape, dim):
    return lax.broadcasted_iota(jnp.int32, shape, dim)


def lane_of(value):
    return iota(value.shape, value.ndim - 1)


def split(value, parts):
    out = []
    for _ in range(parts):
        piece = value.astype(BF16)
        out.append(piece)
        value = value - piece.astype(F32)
    return out


def yz_sum(value):
    lane = lane_of(value)
    y = lane % 8
    z = (lane // 8) % 8
    total = jnp.where(y > 0, pltpu.roll(value, 1, 1), 0.0)
    total = total + jnp.where(y < 7, pltpu.roll(value, 127, 1), 0.0)
    total = total + jnp.where(z > 0, pltpu.roll(value, 8, 1), 0.0)
    return total + jnp.where(z < 7, pltpu.roll(value, 120, 1), 0.0)


def x_sum(tiles, j):
    lane = lane_of(tiles(0))
    left = tiles(j - 1) if j > 0 else jnp.where(lane >= 64, pltpu.roll(tiles(3), 64, 1), 0.0)
    right = tiles(j + 1) if j < 3 else jnp.where(lane < 64, pltpu.roll(tiles(0), 64, 1), 0.0)
    return left + right


def column_select(rows, chip, half, j):
    target = 8 * chip + j + 4 * half
    target = jnp.where(j == 4, jnp.where(half == 0, 8 * chip - 1, 8 * chip + 8), target)
    target = jnp.where(j > 4, -1, target)
    return jnp.where(iota((rows, 128), 1) == target, 1.0, 0.0).astype(BF16)


def edge_gather():
    row = iota((512, 128), 0)
    out = iota((512, 128), 1)
    j, half, z, y = row // 128, (row // 64) % 2, (row // 8) % 8, row % 8
    place = (j + 4 * half) * 8 + y
    hit = ((z == 0) & (out == place)) | ((z == 7) & (out == 64 + place))
    return jnp.where(hit, 1.0, 0.0).astype(BF16)


def edge_spread():
    out = iota((128, 512), 1)
    row = iota((128, 512), 0)
    j, half, z, y = out // 128, (out // 64) % 2, (out // 8) % 8, out % 8
    place = (j + 4 * half) * 8 + y
    hit = ((z == 7) & (row == place)) | ((z == 0) & (row == 64 + place))
    return jnp.where(hit, 1.0, 0.0).astype(BF16)


def kernel(
    v_hbm, k_hbm, slot_hbm, kl_hbm, in_hbm, out_hbm, w_hbm, o_ref,
    v_ref, k_ref, slot_ref, kl_ref, in_ref, out_ref, w_ref,
    pack, msg, got, ninth, vf, vb, svb, onehot, cc, wbuf, ubuf, hbuf, main,
    kt, ka, eok, kzi, hxc, hzc, eo, ezi, ra, bb, ex, ez, ans, ret, turn, places, trip, table,
    load, ready, send1, recv1, sendr, recvr, sendk, recvk, sendz, recvz, send2, recv2,
):
    loads = [
        pltpu.make_async_copy(src, dst, load.at[n])
        for n, (src, dst) in enumerate((
            (v_hbm, v_ref), (in_hbm, in_ref), (out_hbm, out_ref), (kl_hbm, kl_ref), (slot_hbm, slot_ref),
            (w_hbm, w_ref), (k_hbm, k_ref),
        ))
    ]
    loads[0].start()

    me = lax.axis_index("mode")
    zi = lax.axis_index("space")
    nz = lax.axis_size("space")
    chip, core = me // 2, me % 2
    ypos, xpos = chip // SIDE, chip % SIDE

    offsets = [(ky, kx) for ky in range(SIDE) for kx in range(SIDE) if (ky, kx) != (0, 0)]
    offsets.sort(key=lambda o: -(min(o[0], SIDE - o[0]) + min(o[1], SIDE - o[1])))

    def chip_at(ky, kx):
        return lax.rem(ypos + ky, SIDE) * SIDE + lax.rem(xpos + kx, SIDE)

    up, down = lax.rem(zi + 1, nz), lax.rem(zi + nz - 1, nz)

    barrier = pltpu.get_barrier_semaphore()
    twin = chip * 2 + 1 - core
    around = [(n, who, other) for n, other in enumerate((down, up)) for who in (me, twin)]
    for ky, kx in offsets:
        pl.semaphore_signal(barrier, inc=1, device_id=(chip_at(ky, kx) * 2 + core, zi), device_id_type=MESH)
    pl.semaphore_signal(barrier, inc=1, device_id=(twin, zi), device_id_type=MESH)

    odd = lax.rem(zi, 2)

    @pl.when(odd == 0)
    def _():
        for _, who, other in around:
            pl.semaphore_signal(barrier, inc=1, device_id=(who, other), device_id_type=MESH)

    for copy in loads[1:]:
        copy.start()

    for j in range(4, 8):
        ans[pl.ds(32 + j, CHIPS, stride=ANS), :] = jnp.zeros((CHIPS, 128), F32)

    row = iota((256, 128), 0)
    select = column_select(256, (row % 128) // 8, row // 128, row % 8)
    low = iota((128, 128), 1) < 64
    loads[0].wait()
    for m in range(OWN):
        field = v_ref[m].astype(F32).reshape(64, 128)
        field = jnp.concatenate([field, field], axis=0).astype(BF16)
        turned = lax.dot_general(select, field, NT, preferred_element_type=F32)
        turned = jnp.where(low, turned[:128], turned[128:])
        for c in range(CHIPS):
            if m < 8:
                pack[pl.ds(c * 64 + m, 8, stride=8), :] = turned[c * 8 : c * 8 + 8]
            else:
                pack[pl.ds(c * 64 + 40, 8), :] = turned[c * 8 : c * 8 + 8]
    for c in range(CHIPS):
        msg[c] = pack[pl.ds(c * 64, MSG), :].astype(BF16)
    got[core, 0] = msg[chip]

    pl.semaphore_wait(barrier, len(offsets) + 1 + len(around) * odd)

    for ky, kx in offsets:
        target = chip_at(ky, kx)
        pltpu.make_async_remote_copy(
            src_ref=msg.at[target], dst_ref=got.at[core, ky * SIDE + kx], send_sem=send1, recv_sem=recv1.at[ky],
            device_id=(target * 2 + core, zi), device_id_type=MESH,
        ).start()

    @pl.when(odd == 1)
    def _():
        for _, who, other in around:
            pl.semaphore_signal(ready, inc=1, device_id=(who, other), device_id_type=MESH)

    gather_edge = edge_gather()
    spread_edge = edge_spread()
    kt[...] = jnp.zeros_like(kt)
    row16 = iota((16, 128), 0)
    select_k = column_select(16, chip, row16 // 8, row16 % 8)
    loads[6].wait()
    for i in range(TERMS):
        block = k_ref[i].reshape(64, 128)
        block = jnp.concatenate([block, block], axis=0)
        turned = jnp.zeros((16, 128), F32)
        for piece in reversed(split(block, 3)):
            turned = turned + lax.dot_general(select_k, piece, NT, preferred_element_type=F32)
        kt[pl.ds(i, 8, stride=16), :] = jnp.where(low[:8], turned[:8], turned[8:])

    def k_tile(j):
        return kt[j * 16 : j * 16 + 16, :]

    whole = jnp.concatenate([k_tile(j) for j in range(4)], axis=1)
    edge = jnp.zeros((16, 128), F32)
    for piece in reversed(split(whole, 3)):
        edge = edge + jnp.dot(piece, gather_edge, preferred_element_type=F32)
    eok[...] = edge
    k_copies = []
    for n, other in enumerate((down, up)):
        copy = pltpu.make_async_remote_copy(
            src_ref=eok, dst_ref=kzi.at[n], send_sem=sendk.at[n], recv_sem=recvk.at[n],
            device_id=(me, other), device_id_type=MESH,
        )
        k_copies.append(copy)

    @pl.when(odd == 1)
    def _():
        for copy in k_copies:
            copy.start()


    for copy in loads[1:6]:
        copy.wait()
    trip[...] = jnp.full(trip.shape, -1, jnp.int32)
    trip[0:1, 0:TRIPS] = in_ref[...].reshape(1, TRIPS)
    trip[1:2, 0:TRIPS] = out_ref[...].reshape(1, TRIPS)
    trip[2:3, 0:TRIPS] = kl_ref[...].reshape(1, TRIPS)
    table[...] = jnp.zeros(table.shape, F32)
    table[0:1, 0:TRIPS] = w_ref[...].astype(F32).reshape(1, TRIPS)
    slots = jnp.broadcast_to(slot_ref[...].reshape(1, MODES), (16, MODES))
    dev = lax.shift_right_logical(slots * 57, 9)
    kind = slots - dev * OWN
    away_y = (ypos - dev // 8 + SIDE) % SIDE
    away_x = (xpos - (dev // 2) % SIDE + SIDE) % SIDE
    came = (dev % 2) * CHIPS + away_y * SIDE + away_x
    column = jnp.where(kind < 8, came * 8 + kind, 256 + came)
    place = jnp.where(kind < 8, (dev // 2) * 8 + kind, 128 + dev // 2)
    place = jnp.where(dev % 2 == core, place, 240)
    row16m = iota((16, MODES), 0)
    number = jnp.where(row16m < 2, column, place)
    digits = jnp.where(row16m % 2 == 0, lax.shift_right_logical(number, 4), number & 15)
    digits = jnp.where(row16m < 4, digits, 0).astype(F32)
    places[...] = jnp.zeros((16, KPAD), F32)
    places[:, 0:MODES] = digits
    digits = places[...].astype(BF16)
    mode_row = iota((KPAD, TRIPS_PAD), 0)
    hit_in = jnp.where(mode_row == trip[0:1, :], 1.0, 0.0).astype(BF16)
    look_in = jnp.dot(digits, hit_in, preferred_element_type=F32)
    hit_out = jnp.where(mode_row == trip[1:2, :], 1.0, 0.0).astype(BF16)
    look_out = jnp.dot(digits, hit_out, preferred_element_type=F32)
    look_in = look_in.T
    column_t = look_in[:, 0:1] * 16.0 + look_in[:, 1:2]
    place_t = (look_out[2:3] * 16.0 + look_out[3:4]).astype(jnp.int32)
    key_t = jnp.where(place_t < ROWS, trip[2:3, :] * ROWS + place_t, -1)
    trip[3:4, :] = key_t
    lane_number = iota((TRIPS_PAD, KPAD), 1).astype(F32)
    by_column = jnp.where(lane_number == column_t, 1.0, 0.0).astype(BF16)

    @pl.loop(0, TERMS)
    def _(i):
        rows = iota((ROWS, TRIPS_PAD), 0) + i * ROWS
        part = jnp.where(rows == trip[3:4, :], table[0:1, :], 0.0).astype(BF16)
        onehot[pl.ds(pl.multiple_of(i * ROWS, 16), ROWS), :] = part

    vb[288:KPAD, :] = jnp.zeros((KPAD - 288, 768), BF16)
    svb[288:KPAD, :] = jnp.zeros((KPAD - 288, 512), BF16)
    svb[KPAD + 288 :, :] = jnp.zeros((KPAD - 288, 512), BF16)

    inside_up = jnp.where(zi < nz - 1, 1.0, 0.0)
    inside_down = jnp.where(zi > 0, 1.0, 0.0)

    relays = []
    for ky in (0, 1, 3, 2):
        first = 1 if ky == 0 else 0
        here = got.at[core, pl.ds(ky * SIDE + first, SIDE - first)]
        pltpu.make_async_copy(here, here, recv1.at[ky]).wait()
        line = got.at[core, pl.ds(ky * SIDE, SIDE)]
        copy = pltpu.make_async_remote_copy(
            src_ref=line, dst_ref=line, send_sem=sendr.at[ky], recv_sem=recvr.at[ky],
            device_id=(twin, zi), device_id_type=MESH,
        )
        copy.start()
        relays.append(copy)

    def unpack(half):
        most = pl.ds(pl.multiple_of(half * 128, 128), 128)
        rest = pl.ds(pl.multiple_of(256 + half * 16, 16), 16)
        for pair in range(3):
            both = got[half, :, pair * 16 : pair * 16 + 16, :].astype(F32)
            vf[pair * 2, most, :] = both[:, :8, :].reshape(128, 128)
            if pair < 2:
                vf[pair * 2 + 1, most, :] = both[:, 8:, :].reshape(128, 128)
            else:
                ninth[...] = both[:, 8:, :].reshape(128, 128)
        for j in range(5):
            vf[j, rest, :] = ninth[pl.ds(j, 16, stride=8), :]
            vb[most, j * 128 : j * 128 + 128] = vf[j, most, :].astype(BF16)
            vb[rest, j * 128 : j * 128 + 128] = vf[j, rest, :].astype(BF16)
        return most, rest

    most, rest = unpack(core)
    edges = jnp.concatenate(
        [
            jnp.dot(vb[most, 0:512], gather_edge, preferred_element_type=F32),
            jnp.dot(vb[rest, 0:512], gather_edge, preferred_element_type=F32),
            jnp.zeros((16, 128), F32),
        ],
        axis=0,
    )
    low80 = iota((80, 128), 1) < 64
    eo[0] = jnp.where(low80, edges[:80], pltpu.roll(edges[80:], 64, 1)).astype(BF16)
    eo[1] = jnp.where(low80, pltpu.roll(edges[:80], 64, 1), edges[80:]).astype(BF16)
    z_copies = []
    for n, who, other in around:
        cross = 0 if who is me else 1
        copy = pltpu.make_async_remote_copy(
            src_ref=eo.at[n], dst_ref=ezi.at[n, core], send_sem=sendz.at[n, cross], recv_sem=recvz.at[n, cross],
            device_id=(who, other), device_id_type=MESH,
        )
        z_copies.append(copy)

    @pl.when(odd == 1)
    def _():
        for copy in z_copies:
            copy.start()

    p0, p1 = iota((128, 128), 0), iota((128, 128), 1)
    dz, dy = (p0 // 8) % 8 - (p1 // 8) % 8, p0 % 8 - p1 % 8
    near = (p0 // 64 == p1 // 64) & (dz * dz + dy * dy == 1)
    near = jnp.where(near, 1.0, 0.0).astype(BF16)

    def neighbours(rows, low_rows):
        for j in range(4):
            total = jnp.dot(vb[rows, j * 128 : j * 128 + 128], near, preferred_element_type=F32)
            total = total + x_sum(lambda n: vf[n, rows, :], j)
            high, remainder = split(total, 2)
            svb[rows, j * 128 : j * 128 + 128] = high
            svb[low_rows, j * 128 : j * 128 + 128] = remainder

    def shifted_rows(half):
        return (
            pl.ds(pl.multiple_of(KPAD + half * 128, 128), 128),
            pl.ds(pl.multiple_of(KPAD + 256 + half * 16, 16), 16),
        )

    low_most, low_rest = shifted_rows(core)
    neighbours(most, low_most)
    neighbours(rest, low_rest)

    coupling = jnp.dot(onehot[...], by_column, preferred_element_type=F32).astype(BF16)
    cc[:, 0:KPAD] = coupling
    cc[:, KPAD:] = coupling

    for copy in relays:
        copy.wait()
    most, rest = unpack(1 - core)
    low_most, low_rest = shifted_rows(1 - core)
    neighbours(most, low_most)
    neighbours(rest, low_rest)

    @pl.when(odd == 0)
    def _():
        pl.semaphore_wait(ready, len(around))
        for copy in k_copies + z_copies:
            copy.start()

    wbuf[...] = jnp.dot(cc[:, 0:KPAD], vb[:, 0:640], preferred_element_type=F32)

    ubuf[...] = jnp.dot(cc[...], svb[...], preferred_element_type=F32)

    for copy in k_copies:
        copy.wait()
    lane16 = iota((16, 128), 1)
    k_beyond = jnp.where(lane16 < 64, kzi[0] * inside_up, kzi[1] * inside_down)
    hzc[...] = pltpu.roll(edge, 64, 1) + k_beyond
    hxc[...] = jnp.where(lane16 < 64, k_tile(0), k_tile(3)) + k_tile(4)
    spread = jnp.zeros((16, 512), F32)
    for piece in reversed(split(k_beyond, 3)):
        spread = spread + jnp.dot(piece, spread_edge, preferred_element_type=F32)
    for j in range(4):
        total = 6.0 * k_tile(j) + x_sum(k_tile, j) + yz_sum(k_tile(j)) + spread[:, j * 128 : j * 128 + 128]
        if j == 0:
            total = total + jnp.where(lane16 < 64, k_tile(4), 0.0)
        if j == 3:
            total = total + jnp.where(lane16 >= 64, k_tile(4), 0.0)
        ka[j] = total

    @pl.loop(0, ROWS // 16)
    def _(block):
        acc = [jnp.zeros((16, 128), F32) for _ in range(4)]
        mass = [jnp.zeros((16, 128), F32) for _ in range(4)]
        side = jnp.zeros((16, 128), F32)
        for i in range(TERMS):
            at = pl.ds(pl.multiple_of(i * ROWS + block * 16, 16), 16)
            for j in range(4):
                k_row = kt[j * 16 + i : j * 16 + i + 1, :]
                w = wbuf[at, j * 128 : j * 128 + 128]
                acc[j] = acc[j] + ka[j, i : i + 1, :] * w - k_row * ubuf[at, j * 128 : j * 128 + 128]
                mass[j] = mass[j] + k_row * w
            side = side + hxc[i : i + 1, :] * wbuf[at, 512:640]
        here = pl.ds(pl.multiple_of(block * 16, 16), 16)
        for j in range(4):
            ra[j, here, :] = acc[j]
            bb[j, here, :] = mass[j]
        ex[here, :] = side

    lane = iota((ROWS, 128), 1)
    for j in range(4):
        total = ra[j] - x_sum(lambda n: bb[n], j) - yz_sum(bb[j])
        if j == 0:
            total = total - jnp.where(lane < 64, ex[...], 0.0)
        if j == 3:
            total = total - jnp.where(lane >= 64, ex[...], 0.0)
        main[j] = total

    for copy in z_copies:
        copy.wait()
    for half in range(2):
        above = ezi[0, half].astype(F32) * inside_up
        below = ezi[1, half].astype(F32) * inside_down
        one = jnp.where(low80, above, pltpu.roll(below, 64, 1)).astype(BF16)
        two = jnp.where(low80, pltpu.roll(above, 64, 1), below).astype(BF16)
        vb[half * 128 : half * 128 + 80, 640:768] = one
        vb[half * 128 + 80 : half * 128 + 128, 640:768] = two[:48]
        vb[256 + half * 16 : 272 + half * 16, 640:768] = two[48:64]
    hbuf[...] = jnp.dot(cc[:, 0:KPAD], vb[:, 640:768], preferred_element_type=F32)

    for block in range(ROWS // 16):
        ends = jnp.zeros((16, 128), F32)
        for i in range(TERMS):
            at = slice(i * ROWS + block * 16, i * ROWS + block * 16 + 16)
            ends = ends + hzc[i : i + 1, :] * hbuf[at, :]
        ez[block * 16 : block * 16 + 16, :] = ends

    end_parts = jnp.zeros((ROWS, 512), F32)
    for piece in reversed(split(ez[...], 2)):
        end_parts = end_parts + jnp.dot(piece, spread_edge, preferred_element_type=F32)
    for j in range(4):
        total = main[j] - end_parts[:, j * 128 : j * 128 + 128]
        total = 0.5 * total
        for c in range(CHIPS):
            ans[c * ANS + j * 8 : c * ANS + j * 8 + 8, :] = total[c * 8 : c * 8 + 8]
        ans[pl.ds(32 + j, CHIPS, stride=ANS), :] = total[128:ROWS]

    def block_of(c):
        return pl.ds(pl.multiple_of(c * ANS, 8), ANS)

    for ky, kx in offsets:
        target = chip_at(ky, kx)
        pltpu.make_async_remote_copy(
            src_ref=ans.at[block_of(target), :], dst_ref=ret.at[block_of(chip), :], send_sem=send2, recv_sem=recv2,
            device_id=(target * 2 + core, zi), device_id_type=MESH,
        ).start()
    ret[block_of(chip), :] = ans[block_of(chip), :]
    rest = ret.at[pl.ds(0, (CHIPS - 1) * ANS), :]
    pltpu.make_async_copy(rest, rest, recv2).wait()

    low16 = iota((CHIPS, 128), 1) < 64
    for first in range(0, OWN, 2):
        second = min(first + 1, OWN - 1)
        base = first * 64
        for j in range(4):
            one = ret[pl.ds(j * 8 + first if first < 8 else 32 + j, CHIPS, stride=ANS), :]
            two = ret[pl.ds(j * 8 + second if second < 8 else 32 + j, CHIPS, stride=ANS), :]
            turn[pl.ds(base + j, CHIPS, stride=8), :] = jnp.where(low16, one, pltpu.roll(two, 64, 1))
            turn[pl.ds(base + 4 + j, CHIPS, stride=8), :] = jnp.where(low16, pltpu.roll(one, 64, 1), two)
    for first in range(0, OWN, 2):
        turned = turn[first * 64 : first * 64 + 128, :].T
        o_ref[first] = turned[:64].reshape(8, 8, 128)
        if first + 1 < OWN:
            o_ref[first + 1] = turned[64:].reshape(8, 8, 128)

    sent = msg.at[pl.ds(0, CHIPS - 1)]
    pltpu.make_async_copy(sent, sent, send1).wait()
    pltpu.make_async_copy(rest, rest, send2).wait()


def body(mode_field, kl_coeff, mode_slot, trip_kl, trip_in, trip_out, trip_weight):
    vmem = pl.BlockSpec(memory_space=pltpu.VMEM)
    operands = (mode_field, kl_coeff, mode_slot, trip_kl, trip_in, trip_out, trip_weight)
    dma = pltpu.SemaphoreType.DMA
    call = pl.pallas_call(
        kernel,
        out_shape=jax.ShapeDtypeStruct(mode_field.shape, F32),
        in_specs=[pl.BlockSpec(memory_space=pltpu.HBM)] * 7,
        out_specs=vmem,
        scratch_shapes=[
            *(pltpu.VMEM(a.shape, a.dtype) for a in operands),
            pltpu.VMEM((CHIPS * 64, 128), F32),
            pltpu.VMEM((CHIPS, MSG, 128), BF16),
            pltpu.VMEM((2, CHIPS, MSG, 128), BF16),
            pltpu.VMEM((128, 128), F32),
            pltpu.VMEM((5, 288, 128), F32),
            pltpu.VMEM((KPAD, 768), BF16),
            pltpu.VMEM((2 * KPAD, 512), BF16),
            pltpu.VMEM((TERMS * ROWS, TRIPS_PAD), BF16),
            pltpu.VMEM((TERMS * ROWS, 2 * KPAD), BF16),
            pltpu.VMEM((TERMS * ROWS, 640), F32),
            pltpu.VMEM((TERMS * ROWS, 512), F32),
            pltpu.VMEM((TERMS * ROWS, 128), F32),
            pltpu.VMEM((4, ROWS, 128), F32),
            pltpu.VMEM((128, 128), F32),
            pltpu.VMEM((4, 16, 128), F32),
            pltpu.VMEM((16, 128), F32),
            pltpu.VMEM((2, 16, 128), F32),
            pltpu.VMEM((16, 128), F32),
            pltpu.VMEM((16, 128), F32),
            pltpu.VMEM((2, 80, 128), BF16),
            pltpu.VMEM((2, 2, 80, 128), BF16),
            pltpu.VMEM((4, ROWS, 128), F32),
            pltpu.VMEM((4, ROWS, 128), F32),
            pltpu.VMEM((ROWS, 128), F32),
            pltpu.VMEM((ROWS, 128), F32),
            pltpu.VMEM((CHIPS * ANS, 128), F32),
            pltpu.VMEM((CHIPS * ANS, 128), F32),
            pltpu.VMEM((640, 128), F32),
            pltpu.VMEM((16, KPAD), F32),
            pltpu.VMEM((8, TRIPS_PAD), jnp.int32),
            pltpu.VMEM((8, TRIPS_PAD), F32),
            dma((7,)), pltpu.SemaphoreType.REGULAR, dma, dma((SIDE,)), dma((SIDE,)), dma((SIDE,)), dma((2,)), dma((2,)), dma((2, 2)), dma((2, 2)), dma, dma,
        ],
        compiler_params=pltpu.CompilerParams(
            collective_id=0, has_side_effects=True, vmem_limit_bytes=40 << 20
        ),
    )
    return call(*(pltpu.with_memory_space_constraint(a, pltpu.HBM) for a in operands))


def solution(mesh):
    placed = (P("mode", "space", None, None), P(None, "space", None, None), P(), P(), P(), P(), P())
    return jax.shard_map(
        body, mesh=mesh, in_specs=placed, out_specs=P("mode", "space", None, None), check_vma=False
    )
```
